256 devices in a mesh: seq: 32 (over x, z_hi, core), exp: 8 (over y, z_lo).
Axes of the slice: x: 4, y: 4, z: 8 (z_hi: 4, z_lo: 2; z = z_hi * 2 + z_lo), core: 2. Of those that a mesh axis runs over, the one named last changes fastest.
Arguments:
- tokens: bfloat16 [61440, 1024], P('seq'), may hold values from -24 to 24
- slot_embed: bfloat16 [1024, 2048], P(None, 'exp'), may hold values from -3 to 3
- w_in: bfloat16 [128, 1024, 4096], P('exp', None, 'seq'), may hold values from -0.375 to 0.375
- w_out: bfloat16 [128, 4096, 1024], P('exp', 'seq'), may hold values from -0.125 to 0.125
Outputs:
- mixed_out: bfloat16 [61440, 1024], P('seq', 'exp')
The draws below stay inside these ranges and needn't reach their ends.
All inputs are finite; a program needn't handle non-finite values.
Results may differ from the reference program's by a relative error of at most 0.012.
Values may be sent and summed in bfloat16 or wider, within the bound.
No kernel may reach another device: no remote copies, remote signals or barrier semaphores. Data moves between devices by JAX's collectives and lax.ppermute only.
A program may use at most 64 MiB of HBM per device.

```python
import math
import jax
import jax.numpy as jnp
from jax import lax

D = 1024
HID = 4096
SLOT_EXP = 16
TOK_DEV = 1920
TOKENS = 61440
EXPERTS = 128
SLOTS = 2048
N_SEQ = 32
N_EXP = 8


def embed_table(key):
    fraction = jnp.arange(SLOTS, dtype=jnp.float32) / max(SLOTS - 1, 1)
    base_scale = 3.0 / math.sqrt(D) * (0.9 + 0.25 * fraction)
    normals = jnp.clip(jax.random.normal(jax.random.fold_in(key, 11), (D, SLOTS), jnp.float32), -6.0, 6.0)
    table = normals * base_scale[None, :]
    return table


def draw_slot_embed(key, part):
    table = embed_table(key)
    return table.astype(jnp.bfloat16)


def draw_tokens(key, part):
    position = jnp.arange(TOKENS, dtype=jnp.float32) / max(TOKENS - 1, 1)
    row_scale = 0.9 + 0.2 * position
    entries = jnp.clip(jax.random.normal(jax.random.fold_in(key, 21), (TOKENS, D), jnp.float32), -6.0, 6.0)
    values = entries * row_scale[:, None]
    return values.astype(jnp.bfloat16)


def steps_of(key, extent, pieces, low, top_value):
    level = 1.0
    for axis_at, shards_of in pieces:
        draws = jax.random.uniform(jax.random.fold_in(jax.random.fold_in(key, 6), axis_at), (shards_of,), jnp.float32, low / len(pieces), top_value / len(pieces))
        level = level * jnp.repeat(jnp.exp(draws), extent[axis_at] // shards_of).reshape((-1,) + (1,) * (len(extent) - 1 - axis_at))
    return level


def scatter_about(own_key, shape, width, reach, pieces=(), kind=jnp.bfloat16):
    factor_of = steps_of(own_key, shape, pieces, -0.22, 0.18) if pieces else 1.0
    values = jax.random.normal(own_key, shape, jnp.float32) * width * factor_of
    return jnp.minimum(jnp.maximum(values, -reach), reach).astype(kind)


def setup_inputs(seed: int = 0) -> dict:
    keys = jax.random.split(jax.random.key(seed), 5)
    return {
        "tokens": draw_tokens(jax.random.fold_in(keys[4], 71), 0),
        "slot_embed": draw_slot_embed(jax.random.fold_in(keys[4], 71), 0),
        "w_in": scatter_about(keys[2], (EXPERTS, D, HID), (D // 4) ** -0.5, 0.375, ((0, 8), (2, 32))),
        "w_out": scatter_about(keys[3], (EXPERTS, HID, D), (HID // 2) ** -0.5, 0.125, ((0, 8), (1, 32))),
    }


def gelu_tanh(values):
    return 0.5 * values * (1.0 + jnp.tanh(0.7978845608028654 * (values + 0.044715 * values * values * values)))


def reference(tokens, slot_embed, w_in, w_out):
    group_size = SLOTS // N_EXP
    blocks = slot_embed.reshape(D, N_EXP, group_size).transpose(1, 0, 2)

    def dispatch_block(embed_block):
        logits = jnp.dot(tokens, embed_block, preferred_element_type=jnp.float32)
        col_peak = jnp.max(logits, axis=0)
        weights = jnp.exp(logits - col_peak[None, :])
        col_total = jnp.sum(weights, axis=0)
        dispatch = (weights / col_total[None, :]).astype(jnp.bfloat16)
        summed = lax.dot_general(dispatch, tokens, (((0,), (0,)), ((), ())), preferred_element_type=jnp.float32)
        return summed.astype(jnp.bfloat16)

    slot_in = lax.map(dispatch_block, blocks).reshape(EXPERTS, SLOT_EXP, D)

    def expert_apply(operands):
        inputs, first, second = operands
        hidden = gelu_tanh(jnp.dot(inputs, first, preferred_element_type=jnp.float32)).astype(jnp.bfloat16)
        return jnp.dot(hidden, second, preferred_element_type=jnp.float32).astype(jnp.bfloat16)

    slot_out = lax.map(expert_apply, (slot_in, w_in, w_out)).reshape(N_EXP, group_size, D)
    row_blocks = tokens.reshape(N_SEQ, TOK_DEV, D)

    def combine_block(row_block):
        logits = jnp.dot(row_block, slot_embed, preferred_element_type=jnp.float32)
        row_peak = jnp.max(logits, axis=1)
        weights = jnp.exp(logits - row_peak[:, None])
        row_total = jnp.sum(weights, axis=1)
        combine = (weights / row_total[:, None]).astype(jnp.bfloat16)
        part_blocks = combine.reshape(TOK_DEV, N_EXP, group_size).astype(jnp.float32)
        group_mix = jnp.einsum("bgs,gsd->bgd", part_blocks, slot_out.astype(jnp.float32)).astype(jnp.bfloat16)
        group_mix = lax.optimization_barrier(group_mix)
        return jnp.sum(group_mix.astype(jnp.float32), axis=1).astype(jnp.bfloat16)

    return lax.map(combine_block, row_blocks).reshape(TOKENS, D)
```

```python
import jax
import jax.numpy as jnp
from jax import lax
from jax.sharding import Mesh, PartitionSpec as P

F32 = jnp.float32
BF16 = jnp.bfloat16
RING = ("x", "zh")
EXP = ("y", "zl")
SWAP = [(0, 1), (1, 0)]


def gelu_tanh(values):
    return (
        0.5
        * values
        * (1.0 + jnp.tanh(0.7978845608028654 * (values + 0.044715 * values * values * values)))
    )


def split3(column):
    high = lax.reduce_precision(column, 8, 7)
    rest = column - high
    mid = lax.reduce_precision(rest, 8, 7)
    return [high, mid, rest - mid]


def pack(total, peak):
    rows = peak.shape[:-1]
    columns = split3(total) + split3(peak)
    fill = jnp.zeros(rows + (128 - len(columns),), F32)
    return jnp.concatenate(columns + [fill], axis=-1).astype(BF16)


def unpack(tail):
    tail = tail.astype(F32)
    total = tail[..., 0:1] + tail[..., 1:2] + tail[..., 2:3]
    peak = tail[..., 3:4] + tail[..., 4:5] + tail[..., 5:6]
    return total, peak


def half_of(values, core):
    half = values.shape[0] // 2
    return lax.dynamic_slice_in_dim(values, core * half, half, 0)


def in_order(own, other, core):
    return jnp.where(
        core == 0, jnp.concatenate([own, other], 0), jnp.concatenate([other, own], 0)
    )


def on_device(tokens, slot_embed, w_in, w_out):
    experts_here = w_in.shape[0]
    slots = slot_embed.shape[1]
    slot_exp = slots // experts_here
    count, features = tokens.shape
    core = lax.axis_index("core")
    ring = lax.axis_size(RING)
    groups = lax.axis_size(EXP)
    half = slots // 2
    part = half // ring
    width = features // groups

    mine = lax.dynamic_slice_in_dim(slot_embed, core * half, half, 1)
    table_own = lax.all_gather(mine, EXP, axis=1, tiled=True)
    table_other = lax.ppermute(table_own, "core", SWAP)

    logits = lax.dot_general(
        slot_embed, tokens, (((0,), (1,)), ((), ())), preferred_element_type=F32
    )
    peak = jnp.max(logits, axis=1, keepdims=True)
    weights = jnp.exp(logits - peak)
    total = jnp.sum(weights, axis=1, keepdims=True)
    partial_in = jnp.dot(weights.astype(BF16), tokens, preferred_element_type=F32)

    send = jnp.concatenate([partial_in.astype(BF16), pack(total, peak)], axis=1)
    got = lax.ppermute(half_of(send, 1 - core), "core", SWAP)
    got_total, got_peak = unpack(got[:, features:])
    own_total, own_peak = half_of(total, core), half_of(peak, core)
    top = jnp.maximum(own_peak, got_peak)
    own_scale, got_scale = jnp.exp(own_peak - top), jnp.exp(got_peak - top)
    merged = half_of(partial_in, core) * own_scale + got[:, :features].astype(F32) * got_scale
    merged_total = own_total * own_scale + got_total * got_scale

    send = jnp.concatenate([merged.astype(BF16), pack(merged_total, top)], axis=1)
    got = lax.all_to_all(send.reshape(ring, part, -1), RING, 0, 0)
    got_total, got_peak = unpack(got[:, :, features:])
    scale = jnp.exp(got_peak - jnp.max(got_peak, axis=0, keepdims=True))
    summed = jnp.sum(got[:, :, :features].astype(F32) * scale, axis=0)
    slot_part = (summed / jnp.sum(got_total * scale, axis=0)).astype(BF16)
    own = lax.all_to_all(
        jnp.broadcast_to(slot_part[None], (ring, part, features)), RING, 0, 0
    ).reshape(half, features)
    other = lax.ppermute(own, "core", SWAP)
    slot_in = in_order(own, other, core)

    grouped = slot_in.reshape(experts_here, slot_exp, features)
    hidden = gelu_tanh(
        jnp.einsum("esd,edh->esh", grouped, w_in, preferred_element_type=F32)
    ).astype(BF16)
    partial_out = jnp.einsum("esh,ehd->esd", hidden, w_out, preferred_element_type=F32)
    partial_out = partial_out.reshape(slots, features)

    got = lax.ppermute(half_of(partial_out, 1 - core).astype(BF16), "core", SWAP)
    merged = half_of(partial_out, core) + got.astype(F32)
    got = lax.all_to_all(merged.astype(BF16).reshape(ring, part, features), RING, 0, 0)
    out_part = jnp.sum(got.astype(F32), axis=0).astype(BF16)
    got = lax.all_to_all(out_part.reshape(part, groups, width), EXP, 1, 0)
    got = lax.all_to_all(
        jnp.broadcast_to(got[None], (ring, groups, part, width)), RING, 0, 0
    )
    out_own = got.transpose(1, 0, 2, 3).reshape(groups * half, width)
    out_other = lax.ppermute(out_own, "core", SWAP)

    logits_own = jnp.dot(tokens, table_own, preferred_element_type=F32)
    logits_other = jnp.dot(tokens, table_other, preferred_element_type=F32)
    row_peak = jnp.maximum(
        jnp.max(logits_own, axis=1, keepdims=True), jnp.max(logits_other, axis=1, keepdims=True)
    )
    weights_own = jnp.exp(logits_own - row_peak)
    weights_other = jnp.exp(logits_other - row_peak)
    row_total = jnp.sum(weights_own, axis=1, keepdims=True) + jnp.sum(
        weights_other, axis=1, keepdims=True
    )
    mixed = jnp.dot(weights_own.astype(BF16), out_own, preferred_element_type=F32)
    mixed += jnp.dot(weights_other.astype(BF16), out_other, preferred_element_type=F32)
    return (mixed / row_total).astype(BF16)


def solution(mesh):
    grid = Mesh(mesh.devices.reshape(4, 4, 2, 4, 2), ("x", "zh", "core", "y", "zl"))
    seq = ("x", "zh", "core")
    placed = (P(seq, None), P(None, EXP), P(EXP, None, seq), P(EXP, seq, None))
    return jax.shard_map(
        on_device, mesh=grid, in_specs=placed, out_specs=P(seq, EXP), check_vma=False
    )
```

```python
import functools

import jax
import jax.numpy as jnp
from jax import lax
from jax.experimental import pallas as pl
from jax.experimental.pallas import tpu as pltpu
from jax.sharding import Mesh, PartitionSpec as P

F32 = jnp.float32
BF16 = jnp.bfloat16
SEQ = ("x", "zh", "core")
EXP = ("y", "zl")
SWAP = [(0, 1), (1, 0)]
TAIL = 128
VMEM_LIMIT = 16 << 20


def whole():
    return pl.BlockSpec(memory_space=pltpu.VMEM)


def anywhere(count=1):
    return [pl.BlockSpec(memory_space=pl.ANY)] * count


def kept(shape, kind):
    return pltpu.VMEM(shape, kind)


def far_memory(values):
    return pltpu.with_memory_space_constraint(values, pltpu.HBM)


def after(kernel, first, count):
    def ordered(*refs):
        kernel(*refs[:first], *refs[first + count :])

    return ordered


def call(kernel, outs, micros=1, limit=VMEM_LIMIT, **more):
    return pl.pallas_call(
        kernel,
        out_shape=outs,
        compiler_params=pltpu.CompilerParams(vmem_limit_bytes=limit),
        cost_estimate=pl.CostEstimate(
            flops=0, bytes_accessed=micros * 3_000_000, transcendentals=0
        ),
        **more,
    )


def gelu_tanh(values):
    return (
        0.5
        * values
        * (1.0 + jnp.tanh(0.7978845608028654 * (values + 0.044715 * values * values * values)))
    )


def pieces_of(column):
    high = column.astype(BF16).astype(F32)
    rest = column - high
    mid = rest.astype(BF16).astype(F32)
    return [high, mid, rest - mid]


def tail_of(total, peak):
    lane = lax.broadcasted_iota(jnp.int32, (total.shape[0], TAIL), 1)
    tail = jnp.zeros((total.shape[0], TAIL), F32)
    for at, column in enumerate(pieces_of(total) + pieces_of(peak)):
        tail = jnp.where(lane == at, column, tail)
    return tail


def read_tail(tail):
    total = tail[:, 0:1] + tail[:, 1:2] + tail[:, 2:3]
    peak = tail[:, 3:4] + tail[:, 4:5] + tail[:, 5:6]
    return total, peak


def dispatch_kernel(parts, core, tok_any, embed_any, own, send, tok, embed, logits, full, sems):
    rows = tok.shape[0] // parts
    width = tok.shape[1]
    half = own.shape[0]
    first = pltpu.make_async_copy(embed_any, embed, sems.at[parts])
    first.start()
    copies = []
    for at in range(parts):
        here = pl.ds(at * rows, rows)
        copies.append(pltpu.make_async_copy(tok_any.at[here], tok.at[here], sems.at[at]))
        copies[-1].start()
    first.wait()
    peak = None
    for at in range(parts):
        here = pl.ds(at * rows, rows)
        copies[at].wait()
        block = jnp.dot(tok[here, :], embed[...], preferred_element_type=F32)
        logits[here, :] = block
        top = jnp.max(block, axis=0, keepdims=True)
        peak = top if peak is None else jnp.maximum(peak, top)
    weights = jnp.exp(logits[...] - peak)
    total = jnp.sum(weights, axis=0, keepdims=True)
    full[:, :width] = lax.dot_general(
        weights.astype(BF16), tok[...], (((0,), (0,)), ((), ())), preferred_element_type=F32
    )
    stats = jnp.concatenate([total, peak, jnp.zeros((6, total.shape[1]), F32)], axis=0).T
    full[:, width:] = tail_of(stats[:, 0:1], stats[:, 1:2])
    mine = core[0]
    own[...] = full[pl.ds(pl.multiple_of(mine * half, half), half), :]
    send[...] = full[pl.ds(pl.multiple_of((1 - mine) * half, half), half), :].astype(BF16)


def dispatch(core, tokens, slot_embed, parts=5):
    count, width = tokens.shape
    slots = slot_embed.shape[1]
    shape = (slots // 2, width + TAIL)
    return call(
        functools.partial(dispatch_kernel, parts),
        micros=6,
        outs=[kept(shape, F32), kept(shape, BF16)],
        in_specs=[
            pl.BlockSpec(memory_space=pltpu.SMEM),
            pl.BlockSpec(memory_space=pltpu.HBM),
            pl.BlockSpec(memory_space=pltpu.HBM),
        ],
        out_specs=[whole(), whole()],
        scratch_shapes=[
            pltpu.VMEM(tokens.shape, BF16),
            pltpu.VMEM(slot_embed.shape, BF16),
            pltpu.VMEM((count, slots), F32),
            pltpu.VMEM((slots, width + TAIL), F32),
            pltpu.SemaphoreType.DMA((parts + 1,)),
        ],
    )(core, far_memory(tokens), far_memory(slot_embed))


def merge_kernel(own, got, out):
    width = own.shape[1] - TAIL
    own_total, own_peak = read_tail(own[:, width:])
    got_total, got_peak = read_tail(got[:, width:].astype(F32))
    top = jnp.maximum(own_peak, got_peak)
    own_scale, got_scale = jnp.exp(own_peak - top), jnp.exp(got_peak - top)
    merged = own[:, :width] * own_scale + got[:, :width].astype(F32) * got_scale
    out[:, :width] = merged.astype(BF16)
    out[:, width:] = tail_of(own_total * own_scale + got_total * got_scale, top).astype(BF16)


def merge(own, got):
    return call(
        merge_kernel,
        kept(own.shape, BF16),
        in_specs=[whole(), whole()],
        out_specs=whole(),
    )(own, got)


def reduce_in_kernel(got, out):
    count, rows = got.shape[0], got.shape[1]
    width = got.shape[2] - TAIL
    tails = [read_tail(got[at, :, width:].astype(F32)) for at in range(count)]
    top = functools.reduce(jnp.maximum, [peak for _, peak in tails])
    total = jnp.zeros((rows, 1), F32)
    summed = jnp.zeros((rows, width), F32)
    for at, (part_total, part_peak) in enumerate(tails):
        scale = jnp.exp(part_peak - top)
        total += part_total * scale
        summed += got[at, :, :width].astype(F32) * scale
    result = (summed / total).astype(BF16)
    for at in range(count):
        out[at] = result


def reduce_in(got, wait_for):
    count, rows, wide = got.shape
    return call(
        after(reduce_in_kernel, 1, len(wait_for)),
        kept((count, rows, wide - TAIL), BF16),
        in_specs=[whole()] + anywhere(len(wait_for)),
        out_specs=whole(),
    )(got, *wait_for)


def expert_kernel(slot_exp, half_at, slots, w_in_any, w_out_any, out, w_in, w_out, sems):
    count, _, hid = w_in.shape
    rows = 2 * slot_exp
    copies = []
    for at in range(count):
        expert = half_at[0] * count + at
        copies.append(
            (
                pltpu.make_async_copy(w_in_any.at[expert], w_in.at[at], sems.at[2 * at]),
                pltpu.make_async_copy(w_out_any.at[expert], w_out.at[at], sems.at[2 * at + 1]),
            )
        )
        for copy in copies[at]:
            copy.start()
    for at in range(0, count, 2):
        here = slice(at * slot_exp, at * slot_exp + rows)
        copies[at][0].wait()
        copies[at + 1][0].wait()
        first = jnp.concatenate([w_in[at], w_in[at + 1]], axis=1)
        hidden = gelu_tanh(jnp.dot(slots[here, :], first, preferred_element_type=F32))
        row = lax.broadcasted_iota(jnp.int32, hidden.shape, 0) // slot_exp
        column = lax.broadcasted_iota(jnp.int32, hidden.shape, 1) // hid
        hidden = jnp.where(row == column, hidden, 0.0).astype(BF16)
        copies[at][1].wait()
        copies[at + 1][1].wait()
        second = jnp.concatenate([w_out[at], w_out[at + 1]], axis=0)
        out[here, :] = jnp.dot(hidden, second, preferred_element_type=F32).astype(out.dtype)


def experts(half_at, slots, w_in, w_out, kind, wait_for=()):
    count = w_in.shape[0] // 2
    return call(
        after(functools.partial(expert_kernel, slots.shape[0] // count), 4, len(wait_for)),
        kept(slots.shape, kind),
        micros=3,
        in_specs=[pl.BlockSpec(memory_space=pltpu.SMEM), whole()]
        + [pl.BlockSpec(memory_space=pltpu.HBM)] * 2
        + anywhere(len(wait_for)),
        out_specs=whole(),
        scratch_shapes=[
            pltpu.VMEM((count,) + w_in.shape[1:], BF16),
            pltpu.VMEM((count,) + w_out.shape[1:], BF16),
            pltpu.SemaphoreType.DMA((2 * count,)),
        ],
    )(half_at, slots, far_memory(w_in), far_memory(w_out), *wait_for)


def add_kernel(across, own, got, out):
    rows, wide = out.shape[1], out.shape[2]
    merged = own[...] + got[...].astype(F32)
    for at in range(out.shape[0]):
        down, along = at // across, at % across
        out[at] = merged[down * rows : (down + 1) * rows, along * wide : (along + 1) * wide].astype(BF16)


def add_and_cut(own, got, down, across, wait_for):
    rows, wide = own.shape[0] // down, own.shape[1] // across
    return call(
        after(functools.partial(add_kernel, across), 2, len(wait_for)),
        kept((down * across, rows, wide), BF16),
        in_specs=[whole(), whole()] + anywhere(len(wait_for)),
        out_specs=whole(),
    )(own, got, *wait_for)


def reduce_mid_kernel(down, got, out):
    across, rows, wide = out.shape[1], out.shape[2], out.shape[3]
    n_down = got.shape[0] // across
    n_wide = out.shape[0] // down
    for y in range(across):
        summed = got[y].astype(F32)
        for x in range(1, n_down):
            summed += got[x * across + y].astype(F32)
        for h in range(down):
            for l in range(n_wide):
                out[h * n_wide + l, y] = summed[
                    h * rows : (h + 1) * rows, l * wide : (l + 1) * wide
                ].astype(BF16)


def reduce_mid(got, across, down, n_wide, wait_for):
    rows, wide = got.shape[1] // down, got.shape[2] // n_wide
    return call(
        after(functools.partial(reduce_mid_kernel, down), 1, 1),
        kept((down * n_wide, across, rows, wide), BF16),
        in_specs=[whole(), pl.BlockSpec(memory_space=pltpu.HBM)],
        out_specs=whole(),
    )(got, far_memory(wait_for))


def reduce_out_kernel(down, got, out):
    n_wide = got.shape[0] // down
    for y in range(got.shape[1]):
        for l in range(n_wide):
            summed = got[l, y].astype(F32)
            for h in range(1, down):
                summed += got[h * n_wide + l, y].astype(F32)
            result = summed.astype(BF16)
            for at in range(out.shape[0]):
                out[at, y * n_wide + l] = result


def reduce_out(got, down, copies):
    n_wide = got.shape[0] // down
    return call(
        functools.partial(reduce_out_kernel, down),
        kept((copies, got.shape[1] * n_wide) + got.shape[2:], BF16),
        in_specs=[whole()],
        out_specs=whole(),
    )(got)


def combine_kernel(pieces, core, tok_own, tok_other, *refs):
    own, other = refs[: pieces // 2], refs[pieces // 2 : pieces]
    weights, total, logits, table_own, table_other, sems = refs[pieces:]

    def copies():
        at = 0
        for to, which in ((table_own, own), (table_other, other)):
            start = 0
            for piece in which:
                here = pl.ds(start, piece.shape[0])
                yield start, pltpu.make_async_copy(piece, to.at[here], sems.at[at])
                start += piece.shape[0]
                at += 1

    @pl.when(pl.program_id(0) == 0)
    def _():
        started = [copy for _, copy in copies()]
        for copy in started:
            copy.start()
        for copy in started:
            copy.wait()

    peak = None
    wide = table_own.shape[2]
    for at in range(table_own.shape[0]):
        block = jnp.dot(tok_own[...], table_own[at], preferred_element_type=F32)
        block += jnp.dot(tok_other[...], table_other[at], preferred_element_type=F32)
        logits[:, at * wide : (at + 1) * wide] = block
        top = jnp.max(block, axis=1, keepdims=True)
        peak = top if peak is None else jnp.maximum(peak, top)
    sums = jnp.zeros_like(peak)
    for at in range(table_own.shape[0]):
        here = slice(at * wide, (at + 1) * wide)
        block = jnp.exp(logits[:, here] - peak)
        weights[:, here] = block.astype(BF16)
        sums += jnp.sum(block, axis=1, keepdims=True)
    total[...] = jnp.broadcast_to(sums, total.shape)


def combine_weights(core, tokens, own, other, wait_for, steps=8):
    count, width = tokens.shape
    blocks = sum(piece.shape[0] for piece in own)
    depth, wide = own[0].shape[1:]
    slots = blocks * wide
    rows = count // steps
    pieces = own + other
    tokens = far_memory(tokens)
    return call(
        after(functools.partial(combine_kernel, len(pieces)), 3 + len(pieces), 1),
        [pltpu.HBM((count, slots), BF16), pltpu.HBM((count, 128), F32)],
        micros=12,
        grid_spec=pltpu.PrefetchScalarGridSpec(
            num_scalar_prefetch=1,
            grid=(steps,),
            in_specs=[
                pl.BlockSpec((rows, width // 2), lambda i, core: (i, core[0])),
                pl.BlockSpec((rows, width // 2), lambda i, core: (i, 1 - core[0])),
            ]
            + anywhere(len(pieces) + 1),
            out_specs=[
                pl.BlockSpec((rows, slots), lambda i, core: (i, 0)),
                pl.BlockSpec((rows, 128), lambda i, core: (i, 0)),
            ],
            scratch_shapes=[
                pltpu.VMEM((rows, slots), F32),
                pltpu.VMEM((blocks, depth, wide), BF16),
                pltpu.VMEM((blocks, depth, wide), BF16),
                pltpu.SemaphoreType.DMA((len(pieces),)),
            ],
        ),
    )(core, tokens, tokens, *pieces, wait_for)


def output_kernel(place, weights, total, own, other, out, table):
    half = own.shape[0] * own.shape[2]
    groups = own.shape[1]

    @pl.when(pl.program_id(0) == 0)
    def _():
        for at in range(groups):
            group = place[1 + at]
            for rows, start in ((own, place[0]), (other, 1 - place[0])):
                block = rows[:, group].astype(F32).reshape(half, own.shape[3])
                here = pl.multiple_of(at * 2 * half + start * half, half)
                table[pl.ds(here, half), :] = block.astype(BF16)

    mixed = jnp.dot(weights[...], table[...], preferred_element_type=F32)
    out[...] = (mixed / total[...]).astype(BF16)


def output(place, weights, total, own, other, steps=5):
    count, slots = weights.shape
    wide = own.shape[3]
    return call(
        output_kernel,
        jax.ShapeDtypeStruct((count, wide), BF16),
        grid=(steps,),
        in_specs=[
            pl.BlockSpec(memory_space=pltpu.SMEM),
            pl.BlockSpec((count // steps, slots), lambda i: (i, 0)),
            pl.BlockSpec((count // steps, wide), lambda i: (i, 0)),
            whole(),
            whole(),
        ],
        out_specs=pl.BlockSpec((count // steps, wide), lambda i: (i, 0)),
        scratch_shapes=[pltpu.VMEM((slots, wide), BF16)],
    )(place, far_memory(weights), far_memory(total), own, other)


def shift(by):
    return [(i, (i + by) % 4) for i in range(4)]


def on_device(tokens, slot_embed, w_in, w_out):
    count, features = tokens.shape
    slots = slot_embed.shape[1]
    core = lax.axis_index("core").reshape(1)
    y, zl = lax.axis_index("y"), lax.axis_index("zl")
    nx, nh, ny, nl = (lax.axis_size(axis) for axis in ("x", "zh", "y", "zl"))
    half = slots // 2
    part = half // (nx * nh)

    mine = lax.dynamic_slice_in_dim(slot_embed, core[0] * (features // 2), features // 2, 0)
    near = lax.ppermute(mine, "zl", SWAP)
    rows_y = jnp.stack([y, y, y - 1, y - 1, y + 1, y + 1, y + 2, y + 2]) % ny
    rows_l = jnp.stack([zl, 1 - zl] * 4)
    place = jnp.concatenate([core, rows_y * nl + rows_l]).astype(jnp.int32)

    own, send = dispatch(core, tokens, slot_embed)
    merged = merge(own, lax.ppermute(send, "core", SWAP))
    here = jnp.stack([mine, near])
    down = lax.ppermute(here, "y", shift(1))
    up = lax.ppermute(here, "y", shift(-1))
    got = lax.all_to_all(merged.reshape(nx * nh, part, -1), ("x", "zh"), 0, 0)
    spread = reduce_in(got, [down, up])
    far = [lax.ppermute(down[:1], "y", shift(1)), lax.ppermute(up[1:], "y", shift(-1))]
    near_table = [here, down, up]
    near_there = [lax.ppermute(piece, "core", SWAP) for piece in near_table]
    slots_own = lax.all_to_all(spread, ("x", "zh"), 0, 0).reshape(half, features)
    slots_other = lax.ppermute(slots_own, "core", SWAP)

    done_own = experts(core, slots_own, w_in, w_out, F32, far + near_there)
    done_other = experts(1 - core, slots_other, w_in, w_out, BF16)
    far_there = [lax.ppermute(piece, "core", SWAP) for piece in far]
    cut = add_and_cut(done_own, lax.ppermute(done_other, "core", SWAP), nx, ny, far_there)

    weights, total = combine_weights(core, tokens, near_table + far, near_there + far_there, cut)

    got = lax.all_to_all(cut, ("x", "y"), 0, 0)
    got = lax.all_to_all(reduce_mid(got, ny, nh, nl, weights), ("zh", "zl"), 0, 0)
    spread = reduce_out(got, nh, nx * nh)
    out_own = lax.all_to_all(spread, ("x", "zh"), 0, 0)
    out_other = lax.ppermute(out_own, "core", SWAP)
    return output(place, weights, total, out_own, out_other)


def solution(mesh):
    grid = Mesh(mesh.devices.reshape(4, 4, 2, 4, 2), ("x", "zh", "core", "y", "zl"))
    placed = (P(SEQ, None), P(None, EXP), P(EXP, None, SEQ), P(EXP, SEQ, None))
    return jax.shard_map(
        on_device, mesh=grid, in_specs=placed, out_specs=P(SEQ, EXP), check_vma=False
    )
```

```python
import functools

import jax
import jax.numpy as jnp
from jax import lax
from jax.experimental import pallas as pl
from jax.experimental.pallas import tpu as pltpu
from jax.sharding import Mesh, PartitionSpec as P

F32 = jnp.float32
BF16 = jnp.bfloat16
SEQ = ("x", "zh", "core")
EXP = ("y", "zl")
SWAP = [(0, 1), (1, 0)]
TAIL = 128
VMEM_LIMIT = 16 << 20


def whole():
    return pl.BlockSpec(memory_space=pltpu.VMEM)


def anywhere(count=1):
    return [pl.BlockSpec(memory_space=pl.ANY)] * count


def kept(shape, kind):
    return pltpu.VMEM(shape, kind)


def far_memory(values):
    return pltpu.with_memory_space_constraint(values, pltpu.HBM)


def after(kernel, first, count):
    def ordered(*refs):
        kernel(*refs[:first], *refs[first + count :])

    return ordered


def call(kernel, outs, micros=1, limit=VMEM_LIMIT, **more):
    return pl.pallas_call(
        kernel,
        out_shape=outs,
        compiler_params=pltpu.CompilerParams(vmem_limit_bytes=limit),
        cost_estimate=pl.CostEstimate(
            flops=0, bytes_accessed=micros * 30_000, transcendentals=0
        ),
        **more,
    )


def gelu_tanh(values):
    return (
        0.5
        * values
        * (1.0 + jnp.tanh(0.7978845608028654 * (values + 0.044715 * values * values * values)))
    )


def pieces_of(column):
    high = column.astype(BF16).astype(F32)
    rest = column - high
    mid = rest.astype(BF16).astype(F32)
    return [high, mid, rest - mid]


def tail_of(total, peak):
    lane = lax.broadcasted_iota(jnp.int32, (total.shape[0], TAIL), 1)
    tail = jnp.zeros((total.shape[0], TAIL), F32)
    for at, column in enumerate(pieces_of(total) + pieces_of(peak)):
        tail = jnp.where(lane == at, column, tail)
    return tail


def read_tail(tail):
    total = tail[:, 0:1] + tail[:, 1:2] + tail[:, 2:3]
    peak = tail[:, 3:4] + tail[:, 4:5] + tail[:, 5:6]
    return total, peak


def dispatch_kernel(parts, core, tok_any, embed_any, own, send, tok, embed, logits, full, sems):
    rows = tok.shape[0] // parts
    width = tok.shape[1]
    half = own.shape[0]
    first = pltpu.make_async_copy(embed_any, embed, sems.at[parts])
    first.start()
    copies = []
    for at in range(parts):
        here = pl.ds(at * rows, rows)
        copies.append(pltpu.make_async_copy(tok_any.at[here], tok.at[here], sems.at[at]))
        copies[-1].start()
    first.wait()
    peak = None
    for at in range(parts):
        here = pl.ds(at * rows, rows)
        copies[at].wait()
        block = jnp.dot(tok[here, :], embed[...], preferred_element_type=F32)
        logits[here, :] = block
        top = jnp.max(block, axis=0, keepdims=True)
        peak = top if peak is None else jnp.maximum(peak, top)
    weights = jnp.exp(logits[...] - peak)
    total = jnp.sum(weights, axis=0, keepdims=True)
    full[:, :width] = lax.dot_general(
        weights.astype(BF16), tok[...], (((0,), (0,)), ((), ())), preferred_element_type=F32
    )
    stats = jnp.concatenate([total, peak, jnp.zeros((6, total.shape[1]), F32)], axis=0).T
    full[:, width:] = tail_of(stats[:, 0:1], stats[:, 1:2])
    mine = core[0]
    own[...] = full[pl.ds(pl.multiple_of(mine * half, half), half), :]
    send[...] = full[pl.ds(pl.multiple_of((1 - mine) * half, half), half), :].astype(BF16)


def dispatch(core, tokens, slot_embed, parts=5):
    count, width = tokens.shape
    slots = slot_embed.shape[1]
    shape = (slots // 2, width + TAIL)
    return call(
        functools.partial(dispatch_kernel, parts),
        micros=6,
        outs=[kept(shape, F32), kept(shape, BF16)],
        in_specs=[
            pl.BlockSpec(memory_space=pltpu.SMEM),
            pl.BlockSpec(memory_space=pltpu.HBM),
            pl.BlockSpec(memory_space=pltpu.HBM),
        ],
        out_specs=[whole(), whole()],
        scratch_shapes=[
            pltpu.VMEM(tokens.shape, BF16),
            pltpu.VMEM(slot_embed.shape, BF16),
            pltpu.VMEM((count, slots), F32),
            pltpu.VMEM((slots, width + TAIL), F32),
            pltpu.SemaphoreType.DMA((parts + 1,)),
        ],
    )(core, far_memory(tokens), far_memory(slot_embed))


def merge_kernel(own, got, out):
    width = own.shape[1] - TAIL
    own_total, own_peak = read_tail(own[:, width:])
    got_total, got_peak = read_tail(got[:, width:].astype(F32))
    top = jnp.maximum(own_peak, got_peak)
    own_scale, got_scale = jnp.exp(own_peak - top), jnp.exp(got_peak - top)
    merged = own[:, :width] * own_scale + got[:, :width].astype(F32) * got_scale
    out[:, :width] = merged.astype(BF16)
    out[:, width:] = tail_of(own_total * own_scale + got_total * got_scale, top).astype(BF16)


def merge(own, got):
    return call(
        merge_kernel,
        kept(own.shape, BF16),
        in_specs=[whole(), whole()],
        out_specs=whole(),
    )(own, got)


def reduce_in_kernel(got, out):
    count, rows = got.shape[0], got.shape[1]
    width = got.shape[2] - TAIL
    tails = [read_tail(got[at, :, width:].astype(F32)) for at in range(count)]
    top = functools.reduce(jnp.maximum, [peak for _, peak in tails])
    total = jnp.zeros((rows, 1), F32)
    summed = jnp.zeros((rows, width), F32)
    for at, (part_total, part_peak) in enumerate(tails):
        scale = jnp.exp(part_peak - top)
        total += part_total * scale
        summed += got[at, :, :width].astype(F32) * scale
    result = (summed / total).astype(BF16)
    for at in range(count):
        out[at] = result


def reduce_in(got, wait_for):
    count, rows, wide = got.shape
    return call(
        after(reduce_in_kernel, 1, len(wait_for)),
        kept((count, rows, wide - TAIL), BF16),
        in_specs=[whole()] + anywhere(len(wait_for)),
        out_specs=whole(),
    )(got, *wait_for)


def expert_kernel(slot_exp, half_at, slots, w_in_any, w_out_any, out, w_in, w_out, sems):
    count, _, hid = w_in.shape
    rows = 2 * slot_exp
    copies = []
    for at in range(count):
        expert = half_at[0] * count + at
        copies.append(
            (
                pltpu.make_async_copy(w_in_any.at[expert], w_in.at[at], sems.at[2 * at]),
                pltpu.make_async_copy(w_out_any.at[expert], w_out.at[at], sems.at[2 * at + 1]),
            )
        )
        for copy in copies[at]:
            copy.start()
    pairs = range(0, count, 2)
    for at in range(count):
        copies[at][0].wait()
    before = []
    for at in pairs:
        first = jnp.concatenate([w_in[at], w_in[at + 1]], axis=1)
        here = slice(at * slot_exp, at * slot_exp + rows)
        before.append(jnp.dot(slots[here, :], first, preferred_element_type=F32))
    row = lax.broadcasted_iota(jnp.int32, before[0].shape, 0) // slot_exp
    column = lax.broadcasted_iota(jnp.int32, before[0].shape, 1) // hid
    hidden = [jnp.where(row == column, gelu_tanh(block), 0.0).astype(BF16) for block in before]
    for at in range(count):
        copies[at][1].wait()
    for at, block in zip(pairs, hidden, strict=True):
        here = slice(at * slot_exp, at * slot_exp + rows)
        second = jnp.concatenate([w_out[at], w_out[at + 1]], axis=0)
        out[here, :] = jnp.dot(block, second, preferred_element_type=F32).astype(out.dtype)


def experts(half_at, slots, w_in, w_out, kind, wait_for=()):
    count = w_in.shape[0] // 2
    return call(
        after(functools.partial(expert_kernel, slots.shape[0] // count), 4, len(wait_for)),
        kept(slots.shape, kind),
        micros=3,
        in_specs=[pl.BlockSpec(memory_space=pltpu.SMEM), whole()]
        + [pl.BlockSpec(memory_space=pltpu.HBM)] * 2
        + anywhere(len(wait_for)),
        out_specs=whole(),
        scratch_shapes=[
            pltpu.VMEM((count,) + w_in.shape[1:], BF16),
            pltpu.VMEM((count,) + w_out.shape[1:], BF16),
            pltpu.SemaphoreType.DMA((2 * count,)),
        ],
    )(half_at, slots, far_memory(w_in), far_memory(w_out), *wait_for)


def weights_kernel(pieces, core, tok, *refs):
    weights, stats, logits, table, sems = refs[pieces:]
    blocks, width, wide = table.shape
    half = width // 2

    @pl.when(pl.program_id(0) == 0)
    def _():
        copies = []
        for which in range(2):
            side = core[0] if which == 0 else 1 - core[0]
            features = pl.ds(pl.multiple_of(side * half, half), half)
            start = 0
            for piece in refs[which * pieces // 2 : (which + 1) * pieces // 2]:
                to = table.at[pl.ds(start, piece.shape[0]), features]
                copies.append(pltpu.make_async_copy(piece, to, sems.at[len(copies)]))
                copies[-1].start()
                start += piece.shape[0]
        for copy in copies:
            copy.wait()

    peaks = None
    for at in range(blocks):
        block = jnp.dot(tok[...], table[at], preferred_element_type=F32)
        logits[:, at * wide : (at + 1) * wide] = block
        for lanes in range(0, wide, 128):
            some = block[:, lanes : lanes + 128]
            peaks = some if peaks is None else jnp.maximum(peaks, some)
    peak = jnp.max(peaks, axis=1, keepdims=True)
    sums = jnp.zeros_like(peaks)
    for lanes in range(0, blocks * wide, 128):
        block = jnp.exp(logits[:, lanes : lanes + 128] - peak)
        weights[:, lanes : lanes + 128] = block.astype(BF16)
        sums += block
    lane = lax.broadcasted_iota(jnp.int32, stats.shape, 1)
    stats[...] = jnp.where(lane < 64, peak, jnp.sum(sums, axis=1, keepdims=True))


def combine_weights(core, tokens, own, other, wait_for, steps=3):
    count, width = tokens.shape
    blocks = sum(piece.shape[0] for piece in own)
    wide = own[0].shape[2]
    rows = count // steps
    pieces = [far_memory(piece) for piece in own + other]
    return call(
        after(functools.partial(weights_kernel, len(pieces)), 2 + len(pieces), len(wait_for)),
        [pltpu.HBM((count, blocks * wide), BF16), pltpu.HBM((count, 128), F32)],
        micros=2 * blocks,
        limit=40 << 20,
        grid_spec=pltpu.PrefetchScalarGridSpec(
            num_scalar_prefetch=1,
            grid=(steps,),
            in_specs=[pl.BlockSpec((rows, width), lambda i, core: (i, 0))]
            + [pl.BlockSpec(memory_space=pltpu.HBM)] * len(pieces)
            + anywhere(len(wait_for)),
            out_specs=[
                pl.BlockSpec((rows, blocks * wide), lambda i, core: (i, 0)),
                pl.BlockSpec((rows, 128), lambda i, core: (i, 0)),
            ],
            scratch_shapes=[
                pltpu.VMEM((rows, blocks * wide), F32),
                pltpu.VMEM((blocks, width, wide), BF16),
                pltpu.SemaphoreType.DMA((len(pieces),)),
            ],
        ),
    )(core, far_memory(tokens), *pieces, *wait_for)


def output_kernel(parts, place, *refs):
    weights, stats = refs[:parts], refs[parts : 2 * parts]
    own, other, out, table = refs[2 * parts :]
    half = own.shape[0] * own.shape[2]
    groups = own.shape[1]

    @pl.when(pl.program_id(0) == 0)
    def _():
        for at in range(groups):
            group = place[1 + at]
            for rows, start in ((own, place[0]), (other, 1 - place[0])):
                block = rows[:, group].astype(F32).reshape(half, own.shape[3])
                here = pl.multiple_of(at * 2 * half + start * half, half)
                table[pl.ds(here, half), :] = block.astype(BF16)

    peaks = [part[:, 0:1] for part in stats]
    top = functools.reduce(jnp.maximum, peaks)
    scales = [jnp.exp(peak - top) for peak in peaks]
    total = sum(part[:, 64:65] * scale for part, scale in zip(stats, scales, strict=True))
    mixed = jnp.zeros(out.shape, F32)
    start = 0
    for part, scale in zip(weights, scales, strict=True):
        rows = table[start : start + part.shape[1], :]
        mixed += jnp.dot(part[...], rows, preferred_element_type=F32) * (scale / total)
        start += part.shape[1]
    out[...] = mixed.astype(BF16)


def output(place, weights, stats, own, other, steps=5):
    count = weights[0].shape[0]
    slots = sum(part.shape[1] for part in weights)
    wide = own.shape[3]
    rows = count // steps
    return call(
        functools.partial(output_kernel, len(weights)),
        jax.ShapeDtypeStruct((count, wide), BF16),
        limit=24 << 20,
        grid=(steps,),
        in_specs=[pl.BlockSpec(memory_space=pltpu.SMEM)]
        + [pl.BlockSpec((rows, part.shape[1]), lambda i: (i, 0)) for part in weights]
        + [pl.BlockSpec((rows, 128), lambda i: (i, 0)) for part in stats]
        + [whole(), whole()],
        out_specs=pl.BlockSpec((rows, wide), lambda i: (i, 0)),
        scratch_shapes=[pltpu.VMEM((slots, wide), BF16)],
    )(place, *map(far_memory, weights), *map(far_memory, stats), own, other)


def shift(by):
    return [(i, (i + by) % 4) for i in range(4)]


def on_device(tokens, slot_embed, w_in, w_out):
    count, features = tokens.shape
    slots = slot_embed.shape[1]
    core = lax.axis_index("core").reshape(1)
    y, zl = lax.axis_index("y"), lax.axis_index("zl")
    nx, nh, ny, nl = (lax.axis_size(axis) for axis in ("x", "zh", "y", "zl"))
    half = slots // 2
    part = half // (nx * nh)

    mine = lax.dynamic_slice_in_dim(slot_embed, core[0] * (features // 2), features // 2, 0)
    near = lax.ppermute(mine, "zl", SWAP)
    rows_y = jnp.stack([y, y, y - 1, y - 1, y + 1, y + 1, y + 2, y + 2]) % ny
    rows_l = jnp.stack([zl, 1 - zl] * 4)
    place = jnp.concatenate([core, rows_y * nl + rows_l]).astype(jnp.int32)

    own, send = dispatch(core, tokens, slot_embed)
    merged = merge(own, lax.ppermute(send, "core", SWAP))
    here = jnp.stack([mine, near])
    here_there = lax.ppermute(here, "core", SWAP)
    down = lax.ppermute(here, "y", shift(1))
    up = lax.ppermute(here, "y", shift(-1))
    got = lax.all_to_all(merged.reshape(nx * nh, part, -1), ("x", "zh"), 0, 0)
    spread = reduce_in(got, [here_there])
    far = [lax.ppermute(down[:1], "y", shift(1)), lax.ppermute(up[1:], "y", shift(-1))]
    first, first_stats = combine_weights(core, tokens, [here], [here_there], [spread] + far)
    far_there = [lax.ppermute(piece, "core", SWAP) for piece in far]
    down_there, up_there = (lax.ppermute(piece, "core", SWAP) for piece in (down, up))
    slots_own = lax.all_to_all(spread, ("x", "zh"), 0, 0).reshape(half, features)
    slots_own, first_stats, down_there, up_there, far_there = lax.optimization_barrier(
        (slots_own, first_stats, down_there, up_there, far_there)
    )
    slots_other = lax.ppermute(slots_own, "core", SWAP)

    done_own = experts(core, slots_own, w_in, w_out, F32)
    done_other = experts(1 - core, slots_other, w_in, w_out, BF16)
    got = lax.ppermute(done_other, "core", SWAP)

    cut = (done_own + got.astype(F32)).astype(BF16)
    cut = cut.reshape(nx, half // nx, ny, features // ny).transpose(0, 2, 1, 3)
    cut = cut.reshape(nx * ny, half // nx, features // ny)
    second, second_stats = combine_weights(core, tokens, [down], [down_there], [cut])
    got = lax.all_to_all(cut, ("x", "y"), 0, 0)
    got, second_stats = lax.optimization_barrier((got, second_stats))
    got = jnp.sum(got.reshape((nx, ny) + got.shape[1:]).astype(F32), axis=0).astype(BF16)
    cut = got.reshape(ny, nh, part, nl, features // (ny * nl)).transpose(1, 3, 0, 2, 4)
    cut = cut.reshape((nh * nl, ny, part, -1))
    third, third_stats = combine_weights(core, tokens, [up], [up_there], [cut])
    got = lax.all_to_all(cut, ("zh", "zl"), 0, 0)
    got, third_stats = lax.optimization_barrier((got, third_stats))
    got = jnp.sum(got.reshape((nh, nl) + got.shape[1:]).astype(F32), axis=0).astype(BF16)
    got = got.transpose(1, 0, 2, 3).reshape((ny * nl,) + got.shape[2:])
    spread = jnp.broadcast_to(got[None], (nx * nh,) + got.shape)
    fourth, fourth_stats = combine_weights(core, tokens, far, far_there, [spread])
    out_own = lax.all_to_all(spread, ("x", "zh"), 0, 0)
    out_own, fourth_stats = lax.optimization_barrier((out_own, fourth_stats))
    out_other = lax.ppermute(out_own, "core", SWAP)
    return output(
        place,
        [first, second, third, fourth],
        [first_stats, second_stats, third_stats, fourth_stats],
        out_own,
        out_other,
    )


def solution(mesh):
    grid = Mesh(mesh.devices.reshape(4, 4, 2, 4, 2), ("x", "zh", "core", "y", "zl"))
    placed = (P(SEQ, None), P(None, EXP), P(EXP, None, SEQ), P(EXP, SEQ, None))
    return jax.shard_map(
        on_device, mesh=grid, in_specs=placed, out_specs=P(SEQ, EXP), check_vma=False
    )
```

```python
import functools

import jax
import jax.numpy as jnp
from jax import lax
from jax.experimental import pallas as pl
from jax.experimental.pallas import tpu as pltpu
from jax.sharding import Mesh, PartitionSpec as P

F32 = jnp.float32
BF16 = jnp.bfloat16
SEQ = ("x", "zh", "core")
EXP = ("y", "zl")
SWAP = [(0, 1), (1, 0)]
TAIL = 128
VMEM_LIMIT = 16 << 20


def whole():
    return pl.BlockSpec(memory_space=pltpu.VMEM)


def anywhere(count=1):
    return [pl.BlockSpec(memory_space=pl.ANY)] * count


def kept(shape, kind):
    return pltpu.VMEM(shape, kind)


def far_memory(values):
    return pltpu.with_memory_space_constraint(values, pltpu.HBM)


def after(kernel, first, count):
    def ordered(*refs):
        kernel(*refs[:first], *refs[first + count :])

    return ordered


def call(kernel, outs, micros=1, limit=VMEM_LIMIT, **more):
    return pl.pallas_call(
        kernel,
        out_shape=outs,
        compiler_params=pltpu.CompilerParams(vmem_limit_bytes=limit),
        cost_estimate=pl.CostEstimate(
            flops=0, bytes_accessed=micros * 30_000, transcendentals=0
        ),
        **more,
    )


def gelu_tanh(values):
    return (
        0.5
        * values
        * (1.0 + jnp.tanh(0.7978845608028654 * (values + 0.044715 * values * values * values)))
    )


def pieces_of(column):
    high = column.astype(BF16).astype(F32)
    rest = column - high
    mid = rest.astype(BF16).astype(F32)
    return [high, mid, rest - mid]


def tail_of(total, peak):
    lane = lax.broadcasted_iota(jnp.int32, (total.shape[0], TAIL), 1)
    tail = jnp.zeros((total.shape[0], TAIL), F32)
    for at, column in enumerate(pieces_of(total) + pieces_of(peak)):
        tail = jnp.where(lane == at, column, tail)
    return tail


def read_tail(tail):
    total = tail[:, 0:1] + tail[:, 1:2] + tail[:, 2:3]
    peak = tail[:, 3:4] + tail[:, 4:5] + tail[:, 5:6]
    return total, peak


def dispatch_kernel(parts, core, tok_any, embed_any, own, send, tok, embed, logits, full, sems):
    rows = tok.shape[0] // parts
    width = tok.shape[1]
    half = own.shape[0]
    first = pltpu.make_async_copy(embed_any, embed, sems.at[parts])
    first.start()
    copies = []
    for at in range(parts):
        here = pl.ds(at * rows, rows)
        copies.append(pltpu.make_async_copy(tok_any.at[here], tok.at[here], sems.at[at]))
        copies[-1].start()
    first.wait()
    peak = None
    for at in range(parts):
        here = pl.ds(at * rows, rows)
        copies[at].wait()
        block = jnp.dot(tok[here, :], embed[...], preferred_element_type=F32)
        logits[here, :] = block
        top = jnp.max(block, axis=0, keepdims=True)
        peak = top if peak is None else jnp.maximum(peak, top)
    weights = jnp.exp(logits[...] - peak)
    total = jnp.sum(weights, axis=0, keepdims=True)
    full[:, :width] = lax.dot_general(
        weights.astype(BF16), tok[...], (((0,), (0,)), ((), ())), preferred_element_type=F32
    )
    stats = jnp.concatenate([total, peak, jnp.zeros((6, total.shape[1]), F32)], axis=0).T
    full[:, width:] = tail_of(stats[:, 0:1], stats[:, 1:2])
    mine = core[0]
    own[...] = full[pl.ds(pl.multiple_of(mine * half, half), half), :]
    send[...] = full[pl.ds(pl.multiple_of((1 - mine) * half, half), half), :].astype(BF16)


def dispatch(core, tokens, slot_embed, parts=5):
    count, width = tokens.shape
    slots = slot_embed.shape[1]
    shape = (slots // 2, width + TAIL)
    return call(
        functools.partial(dispatch_kernel, parts),
        micros=6,
        outs=[kept(shape, F32), kept(shape, BF16)],
        in_specs=[
            pl.BlockSpec(memory_space=pltpu.SMEM),
            pl.BlockSpec(memory_space=pltpu.HBM),
            pl.BlockSpec(memory_space=pltpu.HBM),
        ],
        out_specs=[whole(), whole()],
        scratch_shapes=[
            pltpu.VMEM(tokens.shape, BF16),
            pltpu.VMEM(slot_embed.shape, BF16),
            pltpu.VMEM((count, slots), F32),
            pltpu.VMEM((slots, width + TAIL), F32),
            pltpu.SemaphoreType.DMA((parts + 1,)),
        ],
    )(core, far_memory(tokens), far_memory(slot_embed))


def merge_kernel(own, got, out):
    width = own.shape[1] - TAIL
    own_total, own_peak = read_tail(own[:, width:])
    got_total, got_peak = read_tail(got[:, width:].astype(F32))
    top = jnp.maximum(own_peak, got_peak)
    own_scale, got_scale = jnp.exp(own_peak - top), jnp.exp(got_peak - top)
    merged = own[:, :width] * own_scale + got[:, :width].astype(F32) * got_scale
    out[:, :width] = merged.astype(BF16)
    out[:, width:] = tail_of(own_total * own_scale + got_total * got_scale, top).astype(BF16)


def merge(own, got):
    return call(
        merge_kernel,
        kept(own.shape, BF16),
        in_specs=[whole(), whole()],
        out_specs=whole(),
    )(own, got)


def reduce_in_kernel(got, out):
    count, rows = got.shape[0], got.shape[1]
    width = got.shape[2] - TAIL
    tails = [read_tail(got[at, :, width:].astype(F32)) for at in range(count)]
    top = functools.reduce(jnp.maximum, [peak for _, peak in tails])
    total = jnp.zeros((rows, 1), F32)
    summed = jnp.zeros((rows, width), F32)
    for at, (part_total, part_peak) in enumerate(tails):
        scale = jnp.exp(part_peak - top)
        total += part_total * scale
        summed += got[at, :, :width].astype(F32) * scale
    result = (summed / total).astype(BF16)
    for at in range(count):
        out[at] = result


def reduce_in(got):
    count, rows, wide = got.shape
    return call(
        reduce_in_kernel,
        kept((count, rows, wide - TAIL), BF16),
        in_specs=[whole()],
        out_specs=whole(),
    )(got)


def expert_kernel(slot_exp, half_at, slots, w_in_any, w_out_any, out, w_in, w_out, sems):
    count, _, hid = w_in.shape
    rows = 2 * slot_exp
    copies = []
    for at in range(count):
        expert = half_at[0] * count + at
        copies.append(
            (
                pltpu.make_async_copy(w_in_any.at[expert], w_in.at[at], sems.at[2 * at]),
                pltpu.make_async_copy(w_out_any.at[expert], w_out.at[at], sems.at[2 * at + 1]),
            )
        )
        for copy in copies[at]:
            copy.start()
    pairs = range(0, count, 2)
    for at in range(count):
        copies[at][0].wait()
    before = []
    for at in pairs:
        first = jnp.concatenate([w_in[at], w_in[at + 1]], axis=1)
        here = slice(at * slot_exp, at * slot_exp + rows)
        before.append(jnp.dot(slots[here, :], first, preferred_element_type=F32))
    row = lax.broadcasted_iota(jnp.int32, before[0].shape, 0) // slot_exp
    column = lax.broadcasted_iota(jnp.int32, before[0].shape, 1) // hid
    hidden = [jnp.where(row == column, gelu_tanh(block), 0.0).astype(BF16) for block in before]
    for at in range(count):
        copies[at][1].wait()
    for at, block in zip(pairs, hidden, strict=True):
        here = slice(at * slot_exp, at * slot_exp + rows)
        second = jnp.concatenate([w_out[at], w_out[at + 1]], axis=0)
        out[here, :] = jnp.dot(block, second, preferred_element_type=F32).astype(out.dtype)


def experts(half_at, slots, w_in, w_out, kind, wait_for=()):
    count = w_in.shape[0] // 2
    return call(
        after(functools.partial(expert_kernel, slots.shape[0] // count), 4, len(wait_for)),
        kept(slots.shape, kind),
        micros=3,
        in_specs=[pl.BlockSpec(memory_space=pltpu.SMEM), whole()]
        + [pl.BlockSpec(memory_space=pltpu.HBM)] * 2
        + anywhere(len(wait_for)),
        out_specs=whole(),
        scratch_shapes=[
            pltpu.VMEM((count,) + w_in.shape[1:], BF16),
            pltpu.VMEM((count,) + w_out.shape[1:], BF16),
            pltpu.SemaphoreType.DMA((2 * count,)),
        ],
    )(half_at, slots, far_memory(w_in), far_memory(w_out), *wait_for)


def weights_kernel(pieces, core, tok, *refs):
    earlier = refs[: len(refs) - pieces - 6]
    refs = refs[len(earlier) :]
    weights, one, two, logits, table, sems = refs[pieces:]
    blocks, width, wide = table.shape
    half = width // 2

    @pl.when(pl.program_id(0) == 0)
    def _():
        copies = []
        for which in range(2):
            side = core[0] if which == 0 else 1 - core[0]
            features = pl.ds(pl.multiple_of(side * half, half), half)
            start = 0
            for piece in refs[which * pieces // 2 : (which + 1) * pieces // 2]:
                to = table.at[pl.ds(start, piece.shape[0]), features]
                copies.append(pltpu.make_async_copy(piece, to, sems.at[len(copies)]))
                copies[-1].start()
                start += piece.shape[0]
        for copy in copies:
            copy.wait()

    peaks = None
    for at in range(blocks):
        block = jnp.dot(tok[...], table[at], preferred_element_type=F32)
        logits[:, at * wide : (at + 1) * wide] = block
        for lanes in range(0, wide, 128):
            some = block[:, lanes : lanes + 128]
            peaks = some if peaks is None else jnp.maximum(peaks, some)
    peak = jnp.broadcast_to(jnp.max(peaks, axis=1, keepdims=True), peaks.shape)
    sums = jnp.zeros_like(peaks)
    for lanes in range(0, blocks * wide, 128):
        block = jnp.exp(logits[:, lanes : lanes + 128] - peak)
        weights[:, lanes : lanes + 128] = block.astype(BF16)
        sums += block
    total = jnp.broadcast_to(jnp.sum(sums, axis=1, keepdims=True), peaks.shape)
    if earlier:
        top = jnp.maximum(earlier[0][...], peak)
        before, now = jnp.exp(earlier[0][...] - top), jnp.exp(peak - top)
        total = earlier[1][...] * before + total * now
        one[...], two[...] = before / total, now / total
    else:
        one[...], two[...] = peak, total


def combine_weights(core, tokens, own, other, wait_for, earlier=(), steps=3):
    stats = pl.BlockSpec((tokens.shape[0] // steps, 128), lambda i, core: (i, 0))
    count, width = tokens.shape
    blocks = sum(piece.shape[0] for piece in own)
    wide = own[0].shape[2]
    rows = count // steps
    pieces = [far_memory(piece) for piece in own + other]
    return call(
        after(
            functools.partial(weights_kernel, len(pieces)),
            2 + len(earlier) + len(pieces),
            len(wait_for),
        ),
        [pltpu.HBM((count, blocks * wide), BF16)] + [pltpu.HBM((count, 128), F32)] * 2,
        micros=2 * blocks,
        limit=40 << 20,
        grid_spec=pltpu.PrefetchScalarGridSpec(
            num_scalar_prefetch=1,
            grid=(steps,),
            in_specs=[pl.BlockSpec((rows, width), lambda i, core: (i, 0))]
            + [stats] * len(earlier)
            + [pl.BlockSpec(memory_space=pltpu.HBM)] * len(pieces)
            + anywhere(len(wait_for)),
            out_specs=[
                pl.BlockSpec((rows, blocks * wide), lambda i, core: (i, 0)),
                stats,
                stats,
            ],
            scratch_shapes=[
                pltpu.VMEM((rows, blocks * wide), F32),
                pltpu.VMEM((blocks, width, wide), BF16),
                pltpu.SemaphoreType.DMA((len(pieces),)),
            ],
        ),
    )(core, far_memory(tokens), *map(far_memory, earlier), *pieces, *wait_for)


def output_kernel(parts, steps, place, *refs):
    sources = refs[: 2 * parts]
    own, other, out = refs[2 * parts : 2 * parts + 3]
    landed, (table, sems) = refs[2 * parts + 3 : -2], refs[-2:]
    weights, scales = landed[:parts], landed[parts:]
    half = own.shape[0] * own.shape[2]
    groups = own.shape[1]
    count = out.shape[0] // steps
    copies = []
    for step in range(steps):
        rows = pl.ds(step * count, count)
        for source, to in zip(sources, landed, strict=True):
            copies.append(
                pltpu.make_async_copy(source.at[rows], to.at[rows], sems.at[len(copies)])
            )
            copies[-1].start()
    for at in range(groups):
        group = place[1 + at]
        for rows, start in ((own, place[0]), (other, 1 - place[0])):
            block = rows[:, group].astype(F32).reshape(half, own.shape[3])
            here = pl.multiple_of(at * 2 * half + start * half, half)
            table[pl.ds(here, half), :] = block.astype(BF16)
    for step in range(steps):
        rows = pl.ds(step * count, count)
        for copy in copies[step * 2 * parts : (step + 1) * 2 * parts]:
            copy.wait()
        mixed = jnp.zeros((count, out.shape[1]), F32)
        start = 0
        for part, scale in zip(weights, scales, strict=True):
            slots = table[start : start + part.shape[1], :]
            product = jnp.dot(part[rows, :], slots, preferred_element_type=F32)
            mixed += product * scale[rows, :]
            start += part.shape[1]
        out[rows, :] = mixed.astype(BF16)


def output(place, weights, scales, own, other, steps=5):
    count = weights[0].shape[0]
    slots = sum(part.shape[1] for part in weights)
    wide = own.shape[3]
    parts = len(weights)
    return call(
        functools.partial(output_kernel, parts, steps),
        jax.ShapeDtypeStruct((count, wide), BF16),
        limit=24 << 20,
        in_specs=[pl.BlockSpec(memory_space=pltpu.SMEM)]
        + [pl.BlockSpec(memory_space=pltpu.HBM)] * (2 * parts)
        + [whole(), whole()],
        out_specs=whole(),
        scratch_shapes=[pltpu.VMEM(part.shape, part.dtype) for part in weights + scales]
        + [
            pltpu.VMEM((slots, wide), BF16),
            pltpu.SemaphoreType.DMA((steps * 2 * parts,)),
        ],
    )(place, *map(far_memory, weights + scales), own, other)


def shift(by):
    return [(i, (i + by) % 4) for i in range(4)]


def on_device(tokens, slot_embed, w_in, w_out):
    count, features = tokens.shape
    slots = slot_embed.shape[1]
    core = lax.axis_index("core").reshape(1)
    y, zl = lax.axis_index("y"), lax.axis_index("zl")
    nx, nh, ny, nl = (lax.axis_size(axis) for axis in ("x", "zh", "y", "zl"))
    half = slots // 2
    part = half // (nx * nh)

    mine = lax.dynamic_slice_in_dim(slot_embed, core[0] * (features // 2), features // 2, 0)
    near = lax.ppermute(mine, "zl", SWAP)
    rows_y = jnp.stack([y, y, y - 1, y - 1, y + 1, y + 1, y + 2, y + 2]) % ny
    rows_l = jnp.stack([zl, 1 - zl] * 4)
    place = jnp.concatenate([core, rows_y * nl + rows_l]).astype(jnp.int32)

    own, send = dispatch(core, tokens, slot_embed)
    merged = merge(own, lax.ppermute(send, "core", SWAP))
    near = lax.optimization_barrier((near, merged))[0]
    here = jnp.stack([mine, near])
    down = lax.ppermute(here, "y", shift(1))
    up = lax.ppermute(here, "y", shift(-1))
    got = lax.all_to_all(merged.reshape(nx * nh, part, -1), ("x", "zh"), 0, 0)
    spread = reduce_in(got)
    far = [lax.ppermute(down[:1], "y", shift(1)), lax.ppermute(up[1:], "y", shift(-1))]
    slots_own = lax.all_to_all(spread, ("x", "zh"), 0, 0).reshape(half, features)
    slots_own, far = lax.optimization_barrier((slots_own, far))
    slots_other = lax.ppermute(slots_own, "core", SWAP)

    done_own = experts(core, slots_own, w_in, w_out, F32)
    done_other = experts(1 - core, slots_other, w_in, w_out, BF16)
    table_own = [here, down, up] + far
    table_other = [lax.ppermute(piece, "core", SWAP) for piece in table_own]
    got = lax.ppermute(done_other, "core", SWAP)
    got, table_other = lax.optimization_barrier((got, table_other))

    cut = (done_own + got.astype(F32)).astype(BF16)
    cut = cut.reshape(nx * nh, part, ny * nl, -1).transpose(0, 2, 1, 3)
    cut = cut.reshape((nx * nh * ny * nl, part, -1))
    first, *stats = combine_weights(core, tokens, table_own[:2], table_other[:2], [cut])
    got = lax.all_to_all(cut, ("x", "zh", "y", "zl"), 0, 0)
    got, stats = lax.optimization_barrier((got, stats))
    got = jnp.sum(got.reshape((nx * nh, ny * nl) + got.shape[1:]).astype(F32), axis=0)
    spread = jnp.broadcast_to(got.astype(BF16)[None], (nx * nh,) + got.shape)
    second, *scales = combine_weights(
        core, tokens, table_own[2:], table_other[2:], [spread], earlier=stats
    )
    out_own = lax.all_to_all(spread, ("x", "zh"), 0, 0)
    out_own, scales = lax.optimization_barrier((out_own, scales))
    out_other = lax.ppermute(out_own, "core", SWAP)
    return output(place, [first, second], scales, out_own, out_other)


def solution(mesh):
    grid = Mesh(mesh.devices.reshape(4, 4, 2, 4, 2), ("x", "zh", "core", "y", "zl"))
    placed = (P(SEQ, None), P(None, EXP), P(EXP, None, SEQ), P(EXP, SEQ, None))
    return jax.shard_map(
        on_device, mesh=grid, in_specs=placed, out_specs=P(SEQ, EXP), check_vma=False
    )
```

```python
import functools

import jax
import jax.numpy as jnp
from jax import lax
from jax.experimental import pallas as pl
from jax.experimental.pallas import tpu as pltpu
from jax.sharding import Mesh, PartitionSpec as P

F32 = jnp.float32
BF16 = jnp.bfloat16
SEQ = ("x", "zh", "core")
EXP = ("y", "zl")
SWAP = [(0, 1), (1, 0)]
TAIL = 128
VMEM_LIMIT = 16 << 20


def whole():
    return pl.BlockSpec(memory_space=pltpu.VMEM)


def anywhere(count=1):
    return [pl.BlockSpec(memory_space=pl.ANY)] * count


def kept(shape, kind):
    return pltpu.VMEM(shape, kind)


def far_memory(values):
    return pltpu.with_memory_space_constraint(values, pltpu.HBM)


def after(kernel, first, count):
    def ordered(*refs):
        kernel(*refs[:first], *refs[first + count :])

    return ordered


def call(kernel, outs, micros=1, limit=VMEM_LIMIT, **more):
    return pl.pallas_call(
        kernel,
        out_shape=outs,
        compiler_params=pltpu.CompilerParams(vmem_limit_bytes=limit),
        cost_estimate=pl.CostEstimate(
            flops=0, bytes_accessed=micros * 30_000, transcendentals=0
        ),
        **more,
    )


def gelu_tanh(values):
    return (
        0.5
        * values
        * (1.0 + jnp.tanh(0.7978845608028654 * (values + 0.044715 * values * values * values)))
    )


def pieces_of(column):
    high = column.astype(BF16).astype(F32)
    rest = column - high
    mid = rest.astype(BF16).astype(F32)
    return [high, mid, rest - mid]


def tail_of(total, peak):
    lane = lax.broadcasted_iota(jnp.int32, (total.shape[0], TAIL), 1)
    tail = jnp.zeros((total.shape[0], TAIL), F32)
    for at, column in enumerate(pieces_of(total) + pieces_of(peak)):
        tail = jnp.where(lane == at, column, tail)
    return tail


def read_tail(tail):
    total = tail[:, 0:1] + tail[:, 1:2] + tail[:, 2:3]
    peak = tail[:, 3:4] + tail[:, 4:5] + tail[:, 5:6]
    return total, peak


def dispatch_kernel(parts, core, tok_any, embed_any, own, send, tok, embed, logits, full, sems):
    rows = tok.shape[0] // parts
    width = tok.shape[1]
    half = own.shape[0]
    first = pltpu.make_async_copy(embed_any, embed, sems.at[parts])
    first.start()
    copies = []
    for at in range(parts):
        here = pl.ds(at * rows, rows)
        copies.append(pltpu.make_async_copy(tok_any.at[here], tok.at[here], sems.at[at]))
        copies[-1].start()
    first.wait()
    peak = None
    for at in range(parts):
        here = pl.ds(at * rows, rows)
        copies[at].wait()
        block = jnp.dot(tok[here, :], embed[...], preferred_element_type=F32)
        logits[here, :] = block
        top = jnp.max(block, axis=0, keepdims=True)
        peak = top if peak is None else jnp.maximum(peak, top)
    weights = jnp.exp(logits[...] - peak)
    total = jnp.sum(weights, axis=0, keepdims=True)
    full[:, :width] = lax.dot_general(
        weights.astype(BF16), tok[...], (((0,), (0,)), ((), ())), preferred_element_type=F32
    )
    stats = jnp.concatenate([total, peak, jnp.zeros((6, total.shape[1]), F32)], axis=0).T
    full[:, width:] = tail_of(stats[:, 0:1], stats[:, 1:2])
    mine = core[0]
    own[...] = full[pl.ds(pl.multiple_of(mine * half, half), half), :]
    send[...] = full[pl.ds(pl.multiple_of((1 - mine) * half, half), half), :].astype(BF16)


def dispatch(core, tokens, slot_embed, parts=5):
    count, width = tokens.shape
    slots = slot_embed.shape[1]
    shape = (slots // 2, width + TAIL)
    return call(
        functools.partial(dispatch_kernel, parts),
        micros=6,
        outs=[kept(shape, F32), kept(shape, BF16)],
        in_specs=[
            pl.BlockSpec(memory_space=pltpu.SMEM),
            pl.BlockSpec(memory_space=pltpu.HBM),
            pl.BlockSpec(memory_space=pltpu.HBM),
        ],
        out_specs=[whole(), whole()],
        scratch_shapes=[
            pltpu.VMEM(tokens.shape, BF16),
            pltpu.VMEM(slot_embed.shape, BF16),
            pltpu.VMEM((count, slots), F32),
            pltpu.VMEM((slots, width + TAIL), F32),
            pltpu.SemaphoreType.DMA((parts + 1,)),
        ],
    )(core, far_memory(tokens), far_memory(slot_embed))


def merge_kernel(own, got, out):
    width = own.shape[1] - TAIL
    own_total, own_peak = read_tail(own[:, width:])
    got_total, got_peak = read_tail(got[:, width:].astype(F32))
    top = jnp.maximum(own_peak, got_peak)
    own_scale, got_scale = jnp.exp(own_peak - top), jnp.exp(got_peak - top)
    merged = own[:, :width] * own_scale + got[:, :width].astype(F32) * got_scale
    out[:, :width] = merged.astype(BF16)
    out[:, width:] = tail_of(own_total * own_scale + got_total * got_scale, top).astype(BF16)


def merge(own, got):
    return call(
        merge_kernel,
        kept(own.shape, BF16),
        in_specs=[whole(), whole()],
        out_specs=whole(),
    )(own, got)


def reduce_in_kernel(got, out):
    count, rows = got.shape[0], got.shape[1]
    width = got.shape[2] - TAIL
    tails = [read_tail(got[at, :, width:].astype(F32)) for at in range(count)]
    top = functools.reduce(jnp.maximum, [peak for _, peak in tails])
    total = jnp.zeros((rows, 1), F32)
    summed = jnp.zeros((rows, width), F32)
    for at, (part_total, part_peak) in enumerate(tails):
        scale = jnp.exp(part_peak - top)
        total += part_total * scale
        summed += got[at, :, :width].astype(F32) * scale
    result = (summed / total).astype(BF16)
    for at in range(count):
        out[at] = result


def reduce_in(got):
    count, rows, wide = got.shape
    return call(
        reduce_in_kernel,
        kept((count, rows, wide - TAIL), BF16),
        in_specs=[whole()],
        out_specs=whole(),
    )(got)


def expert_kernel(slot_exp, half_at, slots, w_in_any, w_out_any, out, w_in, w_out, sems):
    count, _, hid = w_in.shape
    rows = 2 * slot_exp
    copies = []
    for at in range(count):
        expert = half_at[0] * count + at
        copies.append(
            (
                pltpu.make_async_copy(w_in_any.at[expert], w_in.at[at], sems.at[2 * at]),
                pltpu.make_async_copy(w_out_any.at[expert], w_out.at[at], sems.at[2 * at + 1]),
            )
        )
    for which in range(2):
        for pair in copies:
            pair[which].start()
    pairs = range(0, count, 2)
    for at in range(count):
        copies[at][0].wait()
    before = []
    for at in pairs:
        first = jnp.concatenate([w_in[at], w_in[at + 1]], axis=1)
        here = slice(at * slot_exp, at * slot_exp + rows)
        before.append(jnp.dot(slots[here, :], first, preferred_element_type=F32))
    row = lax.broadcasted_iota(jnp.int32, before[0].shape, 0) // slot_exp
    column = lax.broadcasted_iota(jnp.int32, before[0].shape, 1) // hid
    hidden = [jnp.where(row == column, gelu_tanh(block), 0.0).astype(BF16) for block in before]
    for at in range(count):
        copies[at][1].wait()
    for at, block in zip(pairs, hidden, strict=True):
        here = slice(at * slot_exp, at * slot_exp + rows)
        second = jnp.concatenate([w_out[at], w_out[at + 1]], axis=0)
        out[here, :] = jnp.dot(block, second, preferred_element_type=F32).astype(out.dtype)


def experts(half_at, slots, w_in, w_out, kind, wait_for=()):
    count = w_in.shape[0] // 2
    return call(
        after(functools.partial(expert_kernel, slots.shape[0] // count), 4, len(wait_for)),
        kept(slots.shape, kind),
        micros=3,
        in_specs=[pl.BlockSpec(memory_space=pltpu.SMEM), whole()]
        + [pl.BlockSpec(memory_space=pltpu.HBM)] * 2
        + anywhere(len(wait_for)),
        out_specs=whole(),
        scratch_shapes=[
            pltpu.VMEM((count,) + w_in.shape[1:], BF16),
            pltpu.VMEM((count,) + w_out.shape[1:], BF16),
            pltpu.SemaphoreType.DMA((2 * count,)),
        ],
    )(half_at, slots, far_memory(w_in), far_memory(w_out), *wait_for)


def weights_kernel(pieces, core, tok, *refs):
    earlier = refs[: len(refs) - pieces - 6]
    refs = refs[len(earlier) :]
    weights, one, two, logits, table, sems = refs[pieces:]
    blocks, width, wide = table.shape
    half = width // 2

    @pl.when(pl.program_id(0) == 0)
    def _():
        copies = []
        for which in range(2):
            side = core[0] if which == 0 else 1 - core[0]
            features = pl.ds(pl.multiple_of(side * half, half), half)
            start = 0
            for piece in refs[which * pieces // 2 : (which + 1) * pieces // 2]:
                to = table.at[pl.ds(start, piece.shape[0]), features]
                copies.append(pltpu.make_async_copy(piece, to, sems.at[len(copies)]))
                copies[-1].start()
                start += piece.shape[0]
        for copy in copies:
            copy.wait()

    peaks = None
    for at in range(blocks):
        block = jnp.dot(tok[...], table[at], preferred_element_type=F32)
        logits[:, at * wide : (at + 1) * wide] = block
        for lanes in range(0, wide, 128):
            some = block[:, lanes : lanes + 128]
            peaks = some if peaks is None else jnp.maximum(peaks, some)
    peak = jnp.broadcast_to(jnp.max(peaks, axis=1, keepdims=True), peaks.shape)
    sums = jnp.zeros_like(peaks)
    for lanes in range(0, blocks * wide, 128):
        block = jnp.exp(logits[:, lanes : lanes + 128] - peak)
        weights[:, lanes : lanes + 128] = block.astype(BF16)
        sums += block
    total = jnp.broadcast_to(jnp.sum(sums, axis=1, keepdims=True), peaks.shape)
    if earlier:
        top = jnp.maximum(earlier[0][...], peak)
        before, now = jnp.exp(earlier[0][...] - top), jnp.exp(peak - top)
        total = earlier[1][...] * before + total * now
        one[...], two[...] = before / total, now / total
    else:
        one[...], two[...] = peak, total


def combine_weights(core, tokens, own, other, wait_for, earlier=(), steps=3):
    stats = pl.BlockSpec((tokens.shape[0] // steps, 128), lambda i, core: (i, 0))
    count, width = tokens.shape
    blocks = sum(piece.shape[0] for piece in own)
    wide = own[0].shape[2]
    rows = count // steps
    pieces = [far_memory(piece) for piece in own + other]
    return call(
        after(
            functools.partial(weights_kernel, len(pieces)),
            2 + len(earlier) + len(pieces),
            len(wait_for),
        ),
        [pltpu.HBM((count, blocks * wide), BF16)] + [pltpu.HBM((count, 128), F32)] * 2,
        micros=2 * blocks,
        limit=40 << 20,
        grid_spec=pltpu.PrefetchScalarGridSpec(
            num_scalar_prefetch=1,
            grid=(steps,),
            in_specs=[pl.BlockSpec((rows, width), lambda i, core: (i, 0))]
            + [stats] * len(earlier)
            + [pl.BlockSpec(memory_space=pltpu.HBM)] * len(pieces)
            + anywhere(len(wait_for)),
            out_specs=[
                pl.BlockSpec((rows, blocks * wide), lambda i, core: (i, 0)),
                stats,
                stats,
            ],
            scratch_shapes=[
                pltpu.VMEM((rows, blocks * wide), F32),
                pltpu.VMEM((blocks, width, wide), BF16),
                pltpu.SemaphoreType.DMA((len(pieces),)),
            ],
        ),
    )(core, far_memory(tokens), *map(far_memory, earlier), *pieces, *wait_for)


def output_kernel(parts, steps, place, *refs):
    sources = refs[: 2 * parts]
    own, other, out = refs[2 * parts : 2 * parts + 3]
    landed, (table, sems) = refs[2 * parts + 3 : -2], refs[-2:]
    weights, scales = landed[:parts], landed[parts:]
    half = own.shape[0] * own.shape[2]
    groups = own.shape[1]
    count = out.shape[0] // steps
    copies = []
    for step in range(steps):
        rows = pl.ds(step * count, count)
        for source, to in zip(sources, landed, strict=True):
            copies.append(
                pltpu.make_async_copy(source.at[rows], to.at[rows], sems.at[len(copies)])
            )
            copies[-1].start()
    for at in range(groups):
        group = place[1 + at]
        for rows, start in ((own, place[0]), (other, 1 - place[0])):
            block = rows[:, group].astype(F32).reshape(half, own.shape[3])
            here = pl.multiple_of(at * 2 * half + start * half, half)
            table[pl.ds(here, half), :] = block.astype(BF16)
    for step in range(steps):
        rows = pl.ds(step * count, count)
        for copy in copies[step * 2 * parts : (step + 1) * 2 * parts]:
            copy.wait()
        mixed = jnp.zeros((count, out.shape[1]), F32)
        start = 0
        for part, scale in zip(weights, scales, strict=True):
            slots = table[start : start + part.shape[1], :]
            product = jnp.dot(part[rows, :], slots, preferred_element_type=F32)
            mixed += product * scale[rows, :]
            start += part.shape[1]
        out[rows, :] = mixed.astype(BF16)


def output(place, weights, scales, own, other, steps=5):
    count = weights[0].shape[0]
    slots = sum(part.shape[1] for part in weights)
    wide = own.shape[3]
    parts = len(weights)
    return call(
        functools.partial(output_kernel, parts, steps),
        jax.ShapeDtypeStruct((count, wide), BF16),
        limit=24 << 20,
        in_specs=[pl.BlockSpec(memory_space=pltpu.SMEM)]
        + [pl.BlockSpec(memory_space=pltpu.HBM)] * (2 * parts)
        + [whole(), whole()],
        out_specs=whole(),
        scratch_shapes=[pltpu.VMEM(part.shape, part.dtype) for part in weights + scales]
        + [
            pltpu.VMEM((slots, wide), BF16),
            pltpu.SemaphoreType.DMA((steps * 2 * parts,)),
        ],
    )(place, *map(far_memory, weights + scales), own, other)


def shift(by):
    return [(i, (i + by) % 4) for i in range(4)]


def on_device(tokens, slot_embed, w_in, w_out):
    count, features = tokens.shape
    slots = slot_embed.shape[1]
    core = lax.axis_index("core").reshape(1)
    y, zl = lax.axis_index("y"), lax.axis_index("zl")
    nx, nh, ny, nl = (lax.axis_size(axis) for axis in ("x", "zh", "y", "zl"))
    half = slots // 2
    part = half // (nx * nh)

    mine = lax.dynamic_slice_in_dim(slot_embed, core[0] * (features // 2), features // 2, 0)
    near = lax.ppermute(mine, "zl", SWAP)
    rows_y = jnp.stack([y, y, y - 1, y - 1, y + 1, y + 1, y + 2, y + 2]) % ny
    rows_l = jnp.stack([zl, 1 - zl] * 4)
    place = jnp.concatenate([core, rows_l * ny + rows_y]).astype(jnp.int32)

    own, send = dispatch(core, tokens, slot_embed)
    merged = merge(own, lax.ppermute(send, "core", SWAP))
    near = lax.optimization_barrier((near, merged))[0]
    here = jnp.stack([mine, near])
    down = lax.ppermute(here, "y", shift(1))
    up = lax.ppermute(here, "y", shift(-1))
    got = lax.all_to_all(merged.reshape(nx * nh, part, -1), ("x", "zh"), 0, 0)
    spread = reduce_in(got)
    far = [lax.ppermute(down[:1], "y", shift(1)), lax.ppermute(up[1:], "y", shift(-1))]
    slots_own = lax.all_to_all(spread, ("x", "zh"), 0, 0).reshape(half, features)
    slots_own, far = lax.optimization_barrier((slots_own, far))
    slots_other = lax.ppermute(slots_own, "core", SWAP)

    done_own = experts(core, slots_own, w_in, w_out, F32)
    done_other = experts(1 - core, slots_other, w_in, w_out, BF16)
    table_own = [here, down, up] + far
    table_other = [lax.ppermute(piece, "core", SWAP) for piece in table_own]
    got = lax.ppermute(done_other, "core", SWAP)
    got, table_other = lax.optimization_barrier((got, table_other))

    cut = (done_own + got.astype(F32)).astype(BF16)
    cut = cut.reshape(nx * nh, part, ny, nl, -1).transpose(0, 2, 3, 1, 4)
    cut = cut.reshape((nx * nh * ny, nl, part, -1))
    first, *stats = combine_weights(core, tokens, table_own[:2], table_other[:2], [cut])
    got = lax.all_to_all(cut, ("x", "zh", "y"), 0, 0)
    got, stats = lax.optimization_barrier((got, stats))
    got = jnp.sum(got.reshape((nx * nh, ny) + got.shape[1:]).astype(F32), axis=0)
    got = got.astype(BF16).transpose(1, 0, 2, 3)
    spread = jnp.broadcast_to(got[None], (nx * nh,) + got.shape)
    spread = spread.reshape((nx * nh * nl,) + got.shape[1:])
    second, *scales = combine_weights(
        core, tokens, table_own[2:], table_other[2:], [spread], earlier=stats
    )
    out_own = lax.all_to_all(spread, ("x", "zh", "zl"), 0, 0)
    out_own, scales = lax.optimization_barrier((out_own, scales))
    out_own = out_own.reshape((nx * nh, ny * nl) + out_own.shape[2:])
    out_other = lax.ppermute(out_own, "core", SWAP)
    return output(place, [first, second], scales, out_own, out_other)


def solution(mesh):
    grid = Mesh(mesh.devices.reshape(4, 4, 2, 4, 2), ("x", "zh", "core", "y", "zl"))
    placed = (P(SEQ, None), P(None, EXP), P(EXP, None, SEQ), P(EXP, SEQ, None))
    return jax.shard_map(
        on_device, mesh=grid, in_specs=placed, out_specs=P(SEQ, EXP), check_vma=False
    )
```

```python
import functools

import jax
import jax.numpy as jnp
from jax import lax
from jax.experimental import pallas as pl
from jax.experimental.pallas import tpu as pltpu
from jax.sharding import Mesh, PartitionSpec as P

F32 = jnp.float32
BF16 = jnp.bfloat16
SEQ = ("x", "zh", "core")
EXP = ("y", "zl")
SWAP = [(0, 1), (1, 0)]
TAIL = 128
VMEM_LIMIT = 16 << 20


def whole():
    return pl.BlockSpec(memory_space=pltpu.VMEM)


def anywhere(count=1):
    return [pl.BlockSpec(memory_space=pl.ANY)] * count


def kept(shape, kind):
    return pltpu.VMEM(shape, kind)


def far_memory(values):
    return pltpu.with_memory_space_constraint(values, pltpu.HBM)


def after(kernel, first, count):
    def ordered(*refs):
        kernel(*refs[:first], *refs[first + count :])

    return ordered


def call(kernel, outs, micros=1, limit=VMEM_LIMIT, **more):
    return pl.pallas_call(
        kernel,
        out_shape=outs,
        compiler_params=pltpu.CompilerParams(vmem_limit_bytes=limit),
        cost_estimate=pl.CostEstimate(
            flops=0, bytes_accessed=micros * 30_000, transcendentals=0
        ),
        **more,
    )


def gelu_tanh(values):
    return (
        0.5
        * values
        * (1.0 + jnp.tanh(0.7978845608028654 * (values + 0.044715 * values * values * values)))
    )


def pieces_of(column):
    high = column.astype(BF16).astype(F32)
    rest = column - high
    mid = rest.astype(BF16).astype(F32)
    return [high, mid, rest - mid]


def tail_of(total, peak):
    lane = lax.broadcasted_iota(jnp.int32, (total.shape[0], TAIL), 1)
    tail = jnp.zeros((total.shape[0], TAIL), F32)
    for at, column in enumerate(pieces_of(total) + pieces_of(peak)):
        tail = jnp.where(lane == at, column, tail)
    return tail


def read_tail(tail):
    total = tail[:, 0:1] + tail[:, 1:2] + tail[:, 2:3]
    peak = tail[:, 3:4] + tail[:, 4:5] + tail[:, 5:6]
    return total, peak


def dispatch_kernel(parts, core, tok_any, embed_any, own, send, tok, embed, logits, full, sems):
    rows = tok.shape[0] // parts
    width = tok.shape[1]
    half = own.shape[0]
    first = pltpu.make_async_copy(embed_any, embed, sems.at[parts])
    first.start()
    copies = []
    for at in range(parts):
        here = pl.ds(at * rows, rows)
        copies.append(pltpu.make_async_copy(tok_any.at[here], tok.at[here], sems.at[at]))
        copies[-1].start()
    first.wait()
    peak = None
    for at in range(parts):
        here = pl.ds(at * rows, rows)
        copies[at].wait()
        block = jnp.dot(tok[here, :], embed[...], preferred_element_type=F32)
        logits[here, :] = block
        top = jnp.max(block, axis=0, keepdims=True)
        peak = top if peak is None else jnp.maximum(peak, top)
    weights = jnp.exp(logits[...] - peak)
    total = jnp.sum(weights, axis=0, keepdims=True)
    full[:, :width] = lax.dot_general(
        weights.astype(BF16), tok[...], (((0,), (0,)), ((), ())), preferred_element_type=F32
    )
    stats = jnp.concatenate([total, peak, jnp.zeros((6, total.shape[1]), F32)], axis=0).T
    full[:, width:] = tail_of(stats[:, 0:1], stats[:, 1:2])
    mine = core[0]
    own[...] = full[pl.ds(pl.multiple_of(mine * half, half), half), :]
    send[...] = full[pl.ds(pl.multiple_of((1 - mine) * half, half), half), :].astype(BF16)


def dispatch(core, tokens, slot_embed, parts=5):
    count, width = tokens.shape
    slots = slot_embed.shape[1]
    shape = (slots // 2, width + TAIL)
    return call(
        functools.partial(dispatch_kernel, parts),
        micros=6,
        outs=[kept(shape, F32), kept(shape, BF16)],
        in_specs=[
            pl.BlockSpec(memory_space=pltpu.SMEM),
            pl.BlockSpec(memory_space=pltpu.HBM),
            pl.BlockSpec(memory_space=pltpu.HBM),
        ],
        out_specs=[whole(), whole()],
        scratch_shapes=[
            pltpu.VMEM(tokens.shape, BF16),
            pltpu.VMEM(slot_embed.shape, BF16),
            pltpu.VMEM((count, slots), F32),
            pltpu.VMEM((slots, width + TAIL), F32),
            pltpu.SemaphoreType.DMA((parts + 1,)),
        ],
    )(core, far_memory(tokens), far_memory(slot_embed))


def merge_kernel(own, got, out):
    width = own.shape[1] - TAIL
    own_total, own_peak = read_tail(own[:, width:])
    got_total, got_peak = read_tail(got[:, width:].astype(F32))
    top = jnp.maximum(own_peak, got_peak)
    own_scale, got_scale = jnp.exp(own_peak - top), jnp.exp(got_peak - top)
    merged = own[:, :width] * own_scale + got[:, :width].astype(F32) * got_scale
    out[:, :width] = merged.astype(BF16)
    out[:, width:] = tail_of(own_total * own_scale + got_total * got_scale, top).astype(BF16)


def merge(own, got):
    return call(
        merge_kernel,
        kept(own.shape, BF16),
        in_specs=[whole(), whole()],
        out_specs=whole(),
    )(own, got)


def reduce_in_kernel(got, out):
    count, rows = got.shape[0], got.shape[1]
    width = got.shape[2] - TAIL
    tails = [read_tail(got[at, :, width:].astype(F32)) for at in range(count)]
    top = functools.reduce(jnp.maximum, [peak for _, peak in tails])
    total = jnp.zeros((rows, 1), F32)
    summed = jnp.zeros((rows, width), F32)
    for at, (part_total, part_peak) in enumerate(tails):
        scale = jnp.exp(part_peak - top)
        total += part_total * scale
        summed += got[at, :, :width].astype(F32) * scale
    result = (summed / total).astype(BF16)
    for at in range(count):
        out[at] = result


def reduce_in(got):
    count, rows, wide = got.shape
    return call(
        reduce_in_kernel,
        kept((count, rows, wide - TAIL), BF16),
        in_specs=[whole()],
        out_specs=whole(),
    )(got)


def expert_kernel(slot_exp, half_at, slots, w_in_any, w_out_any, out, w_in, w_out, sems):
    count, _, hid = w_in.shape
    rows = 2 * slot_exp
    copies = []
    for at in range(count):
        expert = half_at[0] * count + at
        copies.append(
            (
                pltpu.make_async_copy(w_in_any.at[expert], w_in.at[at], sems.at[2 * at]),
                pltpu.make_async_copy(w_out_any.at[expert], w_out.at[at], sems.at[2 * at + 1]),
            )
        )
    for which in range(2):
        for pair in copies:
            pair[which].start()
    pairs = range(0, count, 2)
    for at in range(count):
        copies[at][0].wait()
    before = []
    for at in pairs:
        first = jnp.concatenate([w_in[at], w_in[at + 1]], axis=1)
        here = slice(at * slot_exp, at * slot_exp + rows)
        before.append(jnp.dot(slots[here, :], first, preferred_element_type=F32))
    row = lax.broadcasted_iota(jnp.int32, before[0].shape, 0) // slot_exp
    column = lax.broadcasted_iota(jnp.int32, before[0].shape, 1) // hid
    hidden = [jnp.where(row == column, gelu_tanh(block), 0.0).astype(BF16) for block in before]
    for at in range(count):
        copies[at][1].wait()
    for at, block in zip(pairs, hidden, strict=True):
        here = slice(at * slot_exp, at * slot_exp + rows)
        second = jnp.concatenate([w_out[at], w_out[at + 1]], axis=0)
        out[here, :] = jnp.dot(block, second, preferred_element_type=F32).astype(out.dtype)


def experts(half_at, slots, w_in, w_out, kind, wait_for=()):
    count = w_in.shape[0] // 2
    return call(
        after(functools.partial(expert_kernel, slots.shape[0] // count), 4, len(wait_for)),
        kept(slots.shape, kind),
        micros=3,
        in_specs=[pl.BlockSpec(memory_space=pltpu.SMEM), whole()]
        + [pl.BlockSpec(memory_space=pltpu.HBM)] * 2
        + anywhere(len(wait_for)),
        out_specs=whole(),
        scratch_shapes=[
            pltpu.VMEM((count,) + w_in.shape[1:], BF16),
            pltpu.VMEM((count,) + w_out.shape[1:], BF16),
            pltpu.SemaphoreType.DMA((2 * count,)),
        ],
    )(half_at, slots, far_memory(w_in), far_memory(w_out), *wait_for)


def weights_kernel(pieces, core, tok, *refs):
    earlier = refs[:2] if len(refs) == pieces + 7 else ()
    refs = refs[len(earlier) :]
    weights, stats, (logits, table, sems) = refs[pieces], refs[pieces + 1 : -3], refs[-3:]
    blocks, width, wide = table.shape
    half = width // 2

    @pl.when(pl.program_id(0) == 0)
    def _():
        copies = []
        for which in range(2):
            side = core[0] if which == 0 else 1 - core[0]
            features = pl.ds(pl.multiple_of(side * half, half), half)
            start = 0
            for piece in refs[which * pieces // 2 : (which + 1) * pieces // 2]:
                to = table.at[pl.ds(start, piece.shape[0]), features]
                copies.append(pltpu.make_async_copy(piece, to, sems.at[len(copies)]))
                copies[-1].start()
                start += piece.shape[0]
        for copy in copies:
            copy.wait()

    peaks = None
    for at in range(blocks):
        block = jnp.dot(tok[...], table[at], preferred_element_type=F32)
        logits[:, at * wide : (at + 1) * wide] = block
        for lanes in range(0, wide, 128):
            some = block[:, lanes : lanes + 128]
            peaks = some if peaks is None else jnp.maximum(peaks, some)
    peak = jnp.broadcast_to(jnp.max(peaks, axis=1, keepdims=True), peaks.shape)
    sums = jnp.zeros_like(peaks)
    for lanes in range(0, blocks * wide, 128):
        block = jnp.exp(logits[:, lanes : lanes + 128] - peak)
        weights[:, lanes : lanes + 128] = block.astype(BF16)
        sums += block
    total = jnp.broadcast_to(jnp.sum(sums, axis=1, keepdims=True), peaks.shape)
    if earlier:
        top = jnp.maximum(earlier[0][...], peak)
        before, now = jnp.exp(earlier[0][...] - top), jnp.exp(peak - top)
        total = earlier[1][...] * before + total * now
        lane = lax.broadcasted_iota(jnp.int32, peak.shape, 1)
        stats[0][...] = jnp.where(lane < 64, before, now) / total
    else:
        stats[0][...], stats[1][...] = peak, total


def combine_weights(core, tokens, own, other, wait_for, earlier=(), steps=3):
    stats = pl.BlockSpec((tokens.shape[0] // steps, 128), lambda i, core: (i, 0))
    count, width = tokens.shape
    blocks = sum(piece.shape[0] for piece in own)
    wide = own[0].shape[2]
    rows = count // steps
    pieces = [far_memory(piece) for piece in own + other]
    return call(
        after(
            functools.partial(weights_kernel, len(pieces)),
            2 + len(earlier) + len(pieces),
            len(wait_for),
        ),
        [pltpu.HBM((count, blocks * wide), BF16)]
        + [pltpu.HBM((count, 128), F32)] * (1 if earlier else 2),
        micros=2 * blocks,
        limit=40 << 20,
        grid_spec=pltpu.PrefetchScalarGridSpec(
            num_scalar_prefetch=1,
            grid=(steps,),
            in_specs=[pl.BlockSpec((rows, width), lambda i, core: (i, 0))]
            + [stats] * len(earlier)
            + [pl.BlockSpec(memory_space=pltpu.HBM)] * len(pieces)
            + anywhere(len(wait_for)),
            out_specs=[pl.BlockSpec((rows, blocks * wide), lambda i, core: (i, 0))]
            + [stats] * (1 if earlier else 2),
            scratch_shapes=[
                pltpu.VMEM((rows, blocks * wide), F32),
                pltpu.VMEM((blocks, width, wide), BF16),
                pltpu.SemaphoreType.DMA((len(pieces),)),
            ],
        ),
    )(core, far_memory(tokens), *map(far_memory, earlier), *pieces, *wait_for)


def output_kernel(parts, steps, place, *refs):
    sources = refs[: parts + 1]
    own, other, out = refs[parts + 1 : parts + 4]
    landed, (table, sems) = refs[parts + 4 : -2], refs[-2:]
    weights, scale = landed[:parts], landed[parts]
    half = own.shape[0] * own.shape[2]
    groups = own.shape[1]
    count = out.shape[0] // steps
    copies = []
    for step in range(steps):
        rows = pl.ds(step * count, count)
        for source, to in zip(sources, landed, strict=True):
            copies.append(
                pltpu.make_async_copy(source.at[rows], to.at[rows], sems.at[len(copies)])
            )
            copies[-1].start()
    for at in range(groups):
        group = place[1 + at]
        for rows, start in ((own, place[0]), (other, 1 - place[0])):
            block = rows[:, group].astype(F32).reshape(half, own.shape[3])
            here = pl.multiple_of(at * 2 * half + start * half, half)
            table[pl.ds(here, half), :] = block.astype(BF16)
    for step in range(steps):
        rows = pl.ds(step * count, count)
        for copy in copies[step * (parts + 1) : (step + 1) * (parts + 1)]:
            copy.wait()
        mixed = jnp.zeros((count, out.shape[1]), F32)
        start = 0
        for at, part in enumerate(weights):
            slots = table[start : start + part.shape[1], :]
            product = jnp.dot(part[rows, :], slots, preferred_element_type=F32)
            mixed += product * scale[rows, 64 * at : 64 * at + 1]
            start += part.shape[1]
        out[rows, :] = mixed.astype(BF16)


def output(place, weights, scales, own, other, steps=5):
    count = weights[0].shape[0]
    slots = sum(part.shape[1] for part in weights)
    wide = own.shape[3]
    parts = len(weights)
    return call(
        functools.partial(output_kernel, parts, steps),
        jax.ShapeDtypeStruct((count, wide), BF16),
        limit=24 << 20,
        in_specs=[pl.BlockSpec(memory_space=pltpu.SMEM)]
        + [pl.BlockSpec(memory_space=pltpu.HBM)] * (parts + 1)
        + [whole(), whole()],
        out_specs=whole(),
        scratch_shapes=[pltpu.VMEM(part.shape, part.dtype) for part in weights + scales]
        + [
            pltpu.VMEM((slots, wide), BF16),
            pltpu.SemaphoreType.DMA((steps * (parts + 1),)),
        ],
    )(place, *map(far_memory, weights + scales), own, other)


def shift(by):
    return [(i, (i + by) % 4) for i in range(4)]


def on_device(tokens, slot_embed, w_in, w_out):
    count, features = tokens.shape
    slots = slot_embed.shape[1]
    core = lax.axis_index("core").reshape(1)
    y, zl = lax.axis_index("y"), lax.axis_index("zl")
    nx, nh, ny, nl = (lax.axis_size(axis) for axis in ("x", "zh", "y", "zl"))
    half = slots // 2
    part = half // (nx * nh)

    mine = lax.dynamic_slice_in_dim(slot_embed, core[0] * (features // 2), features // 2, 0)
    near = lax.ppermute(mine, "zl", SWAP)
    rows_y = jnp.stack([y, y, y - 1, y - 1, y + 1, y + 1, y + 2, y + 2]) % ny
    rows_l = jnp.stack([zl, 1 - zl] * 4)
    place = jnp.concatenate([core, rows_l * ny + rows_y]).astype(jnp.int32)

    own, send = dispatch(core, tokens, slot_embed)
    merged = merge(own, lax.ppermute(send, "core", SWAP))
    near = lax.optimization_barrier((near, merged))[0]
    here = jnp.stack([mine, near])
    down = lax.ppermute(here, "y", shift(1))
    up = lax.ppermute(here, "y", shift(-1))
    got = lax.all_to_all(merged.reshape(nx * nh, part, -1), ("x", "zh"), 0, 0)
    spread = reduce_in(got)
    far = [lax.ppermute(down[:1], "y", shift(1)), lax.ppermute(up[1:], "y", shift(-1))]
    slots_own = lax.all_to_all(spread, ("x", "zh"), 0, 0).reshape(half, features)
    slots_own, far = lax.optimization_barrier((slots_own, far))
    slots_other = lax.ppermute(slots_own, "core", SWAP)

    done_own = experts(core, slots_own, w_in, w_out, F32)
    done_other = experts(1 - core, slots_other, w_in, w_out, BF16)
    table_own = [here, down, up] + far
    table_other = [lax.ppermute(piece, "core", SWAP) for piece in table_own]
    got = lax.ppermute(done_other, "core", SWAP)
    got, table_other = lax.optimization_barrier((got, table_other))

    cut = (done_own + got.astype(F32)).astype(BF16)
    cut = cut.reshape(nx * nh, part, ny, nl, -1).transpose(0, 2, 3, 1, 4)
    cut = cut.reshape((nx * nh * ny, nl, part, -1))
    first, *stats = combine_weights(core, tokens, table_own[:2], table_other[:2], [cut])
    got = lax.all_to_all(cut, ("x", "zh", "y"), 0, 0)
    got, stats = lax.optimization_barrier((got, stats))
    got = jnp.sum(got.reshape((nx * nh, ny) + got.shape[1:]).astype(F32), axis=0)
    got = got.astype(BF16).transpose(1, 0, 2, 3)
    spread = jnp.broadcast_to(got[None], (nx * nh,) + got.shape)
    spread = spread.reshape((nx * nh * nl,) + got.shape[1:])
    second, *scales = combine_weights(
        core, tokens, table_own[2:], table_other[2:], [spread], earlier=stats
    )
    out_own = lax.all_to_all(spread, ("x", "zh", "zl"), 0, 0)
    out_own, scales = lax.optimization_barrier((out_own, scales))
    out_own = out_own.reshape((nx * nh, ny * nl) + out_own.shape[2:])
    out_other = lax.ppermute(out_own, "core", SWAP)
    return output(place, [first, second], scales, out_own, out_other)


def solution(mesh):
    grid = Mesh(mesh.devices.reshape(4, 4, 2, 4, 2), ("x", "zh", "core", "y", "zl"))
    placed = (P(SEQ, None), P(None, EXP), P(EXP, None, SEQ), P(EXP, SEQ, None))
    return jax.shard_map(
        on_device, mesh=grid, in_specs=placed, out_specs=P(SEQ, EXP), check_vma=False
    )
```

```python
import functools

import jax
import jax.numpy as jnp
from jax import lax
from jax.experimental import pallas as pl
from jax.experimental.pallas import tpu as pltpu
from jax.sharding import Mesh, PartitionSpec as P

F32 = jnp.float32
BF16 = jnp.bfloat16
SEQ = ("x", "zh", "core")
EXP = ("y", "zl")
SWAP = [(0, 1), (1, 0)]
TAIL = 128
VMEM_LIMIT = 16 << 20


def whole():
    return pl.BlockSpec(memory_space=pltpu.VMEM)


def anywhere(count=1):
    return [pl.BlockSpec(memory_space=pl.ANY)] * count


def kept(shape, kind):
    return pltpu.VMEM(shape, kind)


def far_memory(values):
    return pltpu.with_memory_space_constraint(values, pltpu.HBM)


def after(kernel, first, count):
    def ordered(*refs):
        kernel(*refs[:first], *refs[first + count :])

    return ordered


def call(kernel, outs, micros=1, limit=VMEM_LIMIT, **more):
    return pl.pallas_call(
        kernel,
        out_shape=outs,
        compiler_params=pltpu.CompilerParams(vmem_limit_bytes=limit),
        cost_estimate=pl.CostEstimate(
            flops=0, bytes_accessed=micros * 30_000, transcendentals=0
        ),
        **more,
    )


def gelu_tanh(values):
    return (
        0.5
        * values
        * (1.0 + jnp.tanh(0.7978845608028654 * (values + 0.044715 * values * values * values)))
    )


def pieces_of(column):
    high = column.astype(BF16).astype(F32)
    rest = column - high
    mid = rest.astype(BF16).astype(F32)
    return [high, mid, rest - mid]


def tail_of(total, peak):
    lane = lax.broadcasted_iota(jnp.int32, (total.shape[0], TAIL), 1)
    tail = jnp.zeros((total.shape[0], TAIL), F32)
    for at, column in enumerate(pieces_of(total) + pieces_of(peak)):
        tail = jnp.where(lane == at, column, tail)
    return tail


def read_tail(tail):
    total = tail[:, 0:1] + tail[:, 1:2] + tail[:, 2:3]
    peak = tail[:, 3:4] + tail[:, 4:5] + tail[:, 5:6]
    return total, peak


def dispatch_kernel(parts, core, tok_any, embed_any, own, send, tok, embed, logits, full, sems):
    rows = tok.shape[0] // parts
    width = tok.shape[1]
    half = own.shape[0]
    first = pltpu.make_async_copy(embed_any, embed, sems.at[parts])
    first.start()
    copies = []
    for at in range(parts):
        here = pl.ds(at * rows, rows)
        copies.append(pltpu.make_async_copy(tok_any.at[here], tok.at[here], sems.at[at]))
        copies[-1].start()
    first.wait()
    peak = None
    for at in range(parts):
        here = pl.ds(at * rows, rows)
        copies[at].wait()
        block = jnp.dot(tok[here, :], embed[...], preferred_element_type=F32)
        logits[here, :] = block
        top = jnp.max(block, axis=0, keepdims=True)
        peak = top if peak is None else jnp.maximum(peak, top)
    weights = jnp.exp(logits[...] - peak)
    total = jnp.sum(weights, axis=0, keepdims=True)
    full[:, :width] = lax.dot_general(
        weights.astype(BF16), tok[...], (((0,), (0,)), ((), ())), preferred_element_type=F32
    )
    stats = jnp.concatenate([total, peak, jnp.zeros((6, total.shape[1]), F32)], axis=0).T
    full[:, width:] = tail_of(stats[:, 0:1], stats[:, 1:2])
    mine = core[0]
    own[...] = full[pl.ds(pl.multiple_of(mine * half, half), half), :]
    send[...] = full[pl.ds(pl.multiple_of((1 - mine) * half, half), half), :].astype(BF16)


def dispatch(core, tokens, slot_embed, parts=6):
    count, width = tokens.shape
    slots = slot_embed.shape[1]
    shape = (slots // 2, width + TAIL)
    return call(
        functools.partial(dispatch_kernel, parts),
        micros=6,
        outs=[kept(shape, F32), kept(shape, BF16)],
        in_specs=[
            pl.BlockSpec(memory_space=pltpu.SMEM),
            pl.BlockSpec(memory_space=pltpu.HBM),
            pl.BlockSpec(memory_space=pltpu.HBM),
        ],
        out_specs=[whole(), whole()],
        scratch_shapes=[
            pltpu.VMEM(tokens.shape, BF16),
            pltpu.VMEM(slot_embed.shape, BF16),
            pltpu.VMEM((count, slots), F32),
            pltpu.VMEM((slots, width + TAIL), F32),
            pltpu.SemaphoreType.DMA((parts + 1,)),
        ],
    )(core, far_memory(tokens), far_memory(slot_embed))


def merge_kernel(own, got, out):
    width = own.shape[1] - TAIL
    own_total, own_peak = read_tail(own[:, width:])
    got_total, got_peak = read_tail(got[:, width:].astype(F32))
    top = jnp.maximum(own_peak, got_peak)
    own_scale, got_scale = jnp.exp(own_peak - top), jnp.exp(got_peak - top)
    merged = own[:, :width] * own_scale + got[:, :width].astype(F32) * got_scale
    out[:, :width] = merged.astype(BF16)
    out[:, width:] = tail_of(own_total * own_scale + got_total * got_scale, top).astype(BF16)


def merge(own, got):
    return call(
        merge_kernel,
        kept(own.shape, BF16),
        in_specs=[whole(), whole()],
        out_specs=whole(),
    )(own, got)


def reduce_in_kernel(got, out):
    count, rows = got.shape[0], got.shape[1]
    width = got.shape[2] - TAIL
    tails = [read_tail(got[at, :, width:].astype(F32)) for at in range(count)]
    top = functools.reduce(jnp.maximum, [peak for _, peak in tails])
    total = jnp.zeros((rows, 1), F32)
    summed = jnp.zeros((rows, width), F32)
    for at, (part_total, part_peak) in enumerate(tails):
        scale = jnp.exp(part_peak - top)
        total += part_total * scale
        summed += got[at, :, :width].astype(F32) * scale
    result = (summed / total).astype(BF16)
    for at in range(count):
        out[at] = result


def reduce_in(got):
    count, rows, wide = got.shape
    return call(
        reduce_in_kernel,
        kept((count, rows, wide - TAIL), BF16),
        in_specs=[whole()],
        out_specs=whole(),
    )(got)


def expert_kernel(slot_exp, half_at, slots, w_in_any, w_out_any, out, w_in, w_out, sems):
    count, _, hid = w_in.shape
    rows = 2 * slot_exp
    copies = []
    for at in range(count):
        expert = half_at[0] * count + at
        copies.append(
            (
                pltpu.make_async_copy(w_in_any.at[expert], w_in.at[at], sems.at[2 * at]),
                pltpu.make_async_copy(w_out_any.at[expert], w_out.at[at], sems.at[2 * at + 1]),
            )
        )
    for which in range(2):
        for pair in copies:
            pair[which].start()
    pairs = range(0, count, 2)
    for at in range(count):
        copies[at][0].wait()
    before = []
    for at in pairs:
        first = jnp.concatenate([w_in[at], w_in[at + 1]], axis=1)
        here = slice(at * slot_exp, at * slot_exp + rows)
        before.append(jnp.dot(slots[here, :], first, preferred_element_type=F32))
    row = lax.broadcasted_iota(jnp.int32, before[0].shape, 0) // slot_exp
    column = lax.broadcasted_iota(jnp.int32, before[0].shape, 1) // hid
    hidden = [jnp.where(row == column, gelu_tanh(block), 0.0).astype(BF16) for block in before]
    for at in range(count):
        copies[at][1].wait()
    for at, block in zip(pairs, hidden, strict=True):
        here = slice(at * slot_exp, at * slot_exp + rows)
        second = jnp.concatenate([w_out[at], w_out[at + 1]], axis=0)
        out[here, :] = jnp.dot(block, second, preferred_element_type=F32).astype(out.dtype)


def experts(half_at, slots, w_in, w_out, kind, wait_for=()):
    count = w_in.shape[0] // 2
    return call(
        after(functools.partial(expert_kernel, slots.shape[0] // count), 4, len(wait_for)),
        kept(slots.shape, kind),
        micros=3,
        in_specs=[pl.BlockSpec(memory_space=pltpu.SMEM), whole()]
        + [pl.BlockSpec(memory_space=pltpu.HBM)] * 2
        + anywhere(len(wait_for)),
        out_specs=whole(),
        scratch_shapes=[
            pltpu.VMEM((count,) + w_in.shape[1:], BF16),
            pltpu.VMEM((count,) + w_out.shape[1:], BF16),
            pltpu.SemaphoreType.DMA((2 * count,)),
        ],
    )(half_at, slots, far_memory(w_in), far_memory(w_out), *wait_for)


def weights_kernel(pieces, core, tok, *refs):
    earlier = refs[:2] if len(refs) == pieces + 7 else ()
    refs = refs[len(earlier) :]
    weights, stats, (logits, table, sems) = refs[pieces], refs[pieces + 1 : -3], refs[-3:]
    blocks, width, wide = table.shape
    half = width // 2

    @pl.when(pl.program_id(0) == 0)
    def _():
        copies = []
        for which in range(2):
            side = core[0] if which == 0 else 1 - core[0]
            features = pl.ds(pl.multiple_of(side * half, half), half)
            start = 0
            for piece in refs[which * pieces // 2 : (which + 1) * pieces // 2]:
                to = table.at[pl.ds(start, piece.shape[0]), features]
                copies.append(pltpu.make_async_copy(piece, to, sems.at[len(copies)]))
                copies[-1].start()
                start += piece.shape[0]
        for copy in copies:
            copy.wait()

    peaks = None
    for at in range(blocks):
        block = jnp.dot(tok[...], table[at], preferred_element_type=F32)
        logits[:, at * wide : (at + 1) * wide] = block
        for lanes in range(0, wide, 128):
            some = block[:, lanes : lanes + 128]
            peaks = some if peaks is None else jnp.maximum(peaks, some)
    peak = jnp.broadcast_to(jnp.max(peaks, axis=1, keepdims=True), peaks.shape)
    sums = jnp.zeros_like(peaks)
    for lanes in range(0, blocks * wide, 128):
        block = jnp.exp(logits[:, lanes : lanes + 128] - peak)
        weights[:, lanes : lanes + 128] = block.astype(BF16)
        sums += block
    total = jnp.broadcast_to(jnp.sum(sums, axis=1, keepdims=True), peaks.shape)
    if earlier:
        top = jnp.maximum(earlier[0][...], peak)
        before, now = jnp.exp(earlier[0][...] - top), jnp.exp(peak - top)
        total = earlier[1][...] * before + total * now
        lane = lax.broadcasted_iota(jnp.int32, peak.shape, 1)
        stats[0][...] = jnp.where(lane < 64, before, now) / total
    else:
        stats[0][...], stats[1][...] = peak, total


def combine_weights(core, tokens, own, other, wait_for, earlier=(), steps=3):
    stats = pl.BlockSpec((tokens.shape[0] // steps, 128), lambda i, core: (i, 0))
    count, width = tokens.shape
    blocks = sum(piece.shape[0] for piece in own)
    wide = own[0].shape[2]
    rows = count // steps
    pieces = [far_memory(piece) for piece in own + other]
    return call(
        after(
            functools.partial(weights_kernel, len(pieces)),
            2 + len(earlier) + len(pieces),
            len(wait_for),
        ),
        [pltpu.HBM((count, blocks * wide), BF16)]
        + [pltpu.HBM((count, 128), F32)] * (1 if earlier else 2),
        micros=2 * blocks,
        limit=40 << 20,
        grid_spec=pltpu.PrefetchScalarGridSpec(
            num_scalar_prefetch=1,
            grid=(steps,),
            in_specs=[pl.BlockSpec((rows, width), lambda i, core: (i, 0))]
            + [stats] * len(earlier)
            + [pl.BlockSpec(memory_space=pltpu.HBM)] * len(pieces)
            + anywhere(len(wait_for)),
            out_specs=[pl.BlockSpec((rows, blocks * wide), lambda i, core: (i, 0))]
            + [stats] * (1 if earlier else 2),
            scratch_shapes=[
                pltpu.VMEM((rows, blocks * wide), F32),
                pltpu.VMEM((blocks, width, wide), BF16),
                pltpu.SemaphoreType.DMA((len(pieces),)),
            ],
        ),
    )(core, far_memory(tokens), *map(far_memory, earlier), *pieces, *wait_for)


def output_kernel(parts, steps, place, *refs):
    sources = refs[: parts + 1]
    own, other, out = refs[parts + 1 : parts + 4]
    landed, (table, sems) = refs[parts + 4 : -2], refs[-2:]
    weights, scale = landed[:parts], landed[parts]
    half = own.shape[0] * own.shape[2]
    groups = own.shape[1]
    count = out.shape[0] // steps
    copies = []
    for step in range(steps):
        rows = pl.ds(step * count, count)
        for source, to in zip(sources, landed, strict=True):
            copies.append(
                pltpu.make_async_copy(source.at[rows], to.at[rows], sems.at[len(copies)])
            )
            copies[-1].start()
    for at in range(groups):
        group = place[1 + at]
        for rows, start in ((own, place[0]), (other, 1 - place[0])):
            block = rows[:, group].astype(F32).reshape(half, own.shape[3])
            here = pl.multiple_of(at * 2 * half + start * half, half)
            table[pl.ds(here, half), :] = block.astype(BF16)
    for step in range(steps):
        rows = pl.ds(step * count, count)
        for copy in copies[step * (parts + 1) : (step + 1) * (parts + 1)]:
            copy.wait()
        mixed = jnp.zeros((count, out.shape[1]), F32)
        start = 0
        for at, part in enumerate(weights):
            slots = table[start : start + part.shape[1], :]
            product = jnp.dot(part[rows, :], slots, preferred_element_type=F32)
            mixed += product * scale[rows, 64 * at : 64 * at + 1]
            start += part.shape[1]
        out[rows, :] = mixed.astype(BF16)


def output(place, weights, scales, own, other, steps=5):
    count = weights[0].shape[0]
    slots = sum(part.shape[1] for part in weights)
    wide = own.shape[3]
    parts = len(weights)
    return call(
        functools.partial(output_kernel, parts, steps),
        jax.ShapeDtypeStruct((count, wide), BF16),
        limit=24 << 20,
        in_specs=[pl.BlockSpec(memory_space=pltpu.SMEM)]
        + [pl.BlockSpec(memory_space=pltpu.HBM)] * (parts + 1)
        + [whole(), whole()],
        out_specs=whole(),
        scratch_shapes=[pltpu.VMEM(part.shape, part.dtype) for part in weights + scales]
        + [
            pltpu.VMEM((slots, wide), BF16),
            pltpu.SemaphoreType.DMA((steps * (parts + 1),)),
        ],
    )(place, *map(far_memory, weights + scales), own, other)


def flip(bits):
    return [(i, i ^ bits) for i in range(4)]


def on_device(tokens, slot_embed, w_in, w_out):
    count, features = tokens.shape
    slots = slot_embed.shape[1]
    core = lax.axis_index("core").reshape(1)
    y, zl = lax.axis_index("y"), lax.axis_index("zl")
    nx, nh, ny, nl = (lax.axis_size(axis) for axis in ("x", "zh", "y", "zl"))
    half = slots // 2
    part = half // (nx * nh)

    mine = lax.dynamic_slice_in_dim(slot_embed, core[0] * (features // 2), features // 2, 0)
    near = lax.ppermute(mine, "zl", SWAP)
    rows_y = jnp.stack([y, y, y ^ 1, y ^ 1, y ^ 3, y ^ 3, y ^ 2, y ^ 2])
    rows_l = jnp.stack([zl, 1 - zl] * 4)
    place = jnp.concatenate([core, rows_l * ny + rows_y]).astype(jnp.int32)

    own, send = dispatch(core, tokens, slot_embed)
    merged = merge(own, lax.ppermute(send, "core", SWAP))
    near = lax.optimization_barrier((near, merged))[0]
    here = jnp.stack([mine, near])
    down = lax.ppermute(here, "y", flip(1))
    up = lax.ppermute(here, "y", flip(3))
    got = lax.all_to_all(merged.reshape(nx * nh, part, -1), ("x", "zh"), 0, 0)
    spread = reduce_in(got)
    far = [lax.ppermute(down[:1], "y", flip(3)), lax.ppermute(up[1:], "y", flip(1))]
    slots_own = lax.all_to_all(spread, ("x", "zh"), 0, 0).reshape(half, features)
    slots_own, far = lax.optimization_barrier((slots_own, far))
    slots_other = lax.ppermute(slots_own, "core", SWAP)

    done_own = experts(core, slots_own, w_in, w_out, F32)
    done_other = experts(1 - core, slots_other, w_in, w_out, BF16)
    table_own = [here, down, up] + far
    table_other = [lax.ppermute(piece, "core", SWAP) for piece in table_own]
    got = lax.ppermute(done_other, "core", SWAP)
    got, table_other = lax.optimization_barrier((got, table_other))

    cut = (done_own + got.astype(F32)).astype(BF16)
    cut = cut.reshape(nx * nh, part, ny, nl, -1).transpose(0, 2, 3, 1, 4)
    cut = cut.reshape((nx * nh * ny, nl, part, -1))
    first, *stats = combine_weights(core, tokens, table_own[:2], table_other[:2], [cut])
    got = lax.all_to_all(cut, ("x", "zh", "y"), 0, 0)
    got, stats = lax.optimization_barrier((got, stats))
    got = jnp.sum(got.reshape((nx * nh, ny) + got.shape[1:]).astype(F32), axis=0)
    got = got.astype(BF16).transpose(1, 0, 2, 3)
    spread = jnp.broadcast_to(got[None], (nx * nh,) + got.shape)
    spread = spread.reshape((nx * nh * nl,) + got.shape[1:])
    second, *scales = combine_weights(
        core, tokens, table_own[2:], table_other[2:], [spread], earlier=stats
    )
    out_own = lax.all_to_all(spread, ("x", "zh", "zl"), 0, 0)
    out_own, scales = lax.optimization_barrier((out_own, scales))
    out_own = out_own.reshape((nx * nh, ny * nl) + out_own.shape[2:])
    out_other = lax.ppermute(out_own, "core", SWAP)
    return output(place, [first, second], scales, out_own, out_other)


def solution(mesh):
    grid = Mesh(mesh.devices.reshape(4, 4, 2, 4, 2), ("x", "zh", "core", "y", "zl"))
    placed = (P(SEQ, None), P(None, EXP), P(EXP, None, SEQ), P(EXP, SEQ, None))
    return jax.shard_map(
        on_device, mesh=grid, in_specs=placed, out_specs=P(SEQ, EXP), check_vma=False
    )
```
